32 devices in a mesh: groups: 2 (over y), scan: 16 (over z, x, core), obj: 1, sub: 1.
Axes of the slice: x: 2, y: 2, z: 4, core: 2. Of those that a mesh axis runs over, the one named last changes fastest.
Arguments:
- object_field: float32 [2, 8192, 512], P(None, ('groups', 'scan'), 'obj'), parts along dimension 1, may hold values from -3 to 3
- probe_field: float32 [4, 256, 256], P('groups'), parts along dimension 0, may hold values from -3 to 3
- intensities: float32 [2, 1, 96, 256, 256], P(('groups', 'obj'), 'sub', 'scan'), parts along dimension 0, may hold values from 0.05 to 0.5
- positions: int32 [2, 1, 96, 2], P(('groups', 'obj'), 'sub', 'scan'), parts along dimension 0, may hold values from 0 to 3839, as said below
- live_counts: int32 [2, 1, 16], P(('groups', 'obj'), 'sub', 'scan'), parts along dimension 0, may hold values from 5 to 6, as said below
Outputs:
- object_grad: float32 [2, 8192, 512], P(None, ('groups', 'scan'), 'obj'), parts along dimension 1
- probe_grad: float32 [4, 256, 256], P('groups'), parts along dimension 0
The draws below stay inside these ranges and needn't reach their ends.
There are 2 independent parts, one for each index of `groups`. The reference program is written for one: setup_inputs(seed, part) draws one part's arguments, and reference() takes and returns one part's arrays. A program takes and returns all parts, laid end to end along the dimension named above; each array names one. Nothing has to cross between parts.
Inputs may be any that keep to these rules, and one draw needn't show every extreme that they name: `positions`: row r lies in band r // 256; the bands of the 6 slots of one device differ pairwise by 2 or more, none exceeds 16 - 2, and slots run in increasing or decreasing band order. Column c of a pattern in stripe o lies from o * 512 to o * 512 + 256. The live slots of a device are its first live_counts ones.
All inputs are finite; a program needn't handle non-finite values.
Results may differ from the reference program's by a relative error of at most 0.0033.
The reference program's roundings to bfloat16 on the way count: a program that leaves them out, or rounds other values in their place, can miss the bound.
Values may be sent and summed in bfloat16 or wider, within the bound.
A program may use at most 64 MiB of HBM per device.

```python
import jax
import jax.numpy as jnp
from jax import lax

PIX = 256
TX = 512
PAT_DEV = 6
OBJ_ROWS = 4096
OBJ_COLS = 512
SCANS = 96
N_SCAN = 16
N_OBJ = 1
N_SUB = 1


def draw_positions(key, part):
    key = jax.random.fold_in(key, 11)
    subkeys = jax.random.split(key, 4)
    device_total = N_OBJ * N_SUB * N_SCAN

    def bands_of_device(device_key):
        shuffled = jax.random.permutation(device_key, N_SCAN - 1 - PAT_DEV) + 1
        picked = jnp.concatenate([jnp.zeros((1,), jnp.int32), shuffled[:PAT_DEV - 1].astype(jnp.int32)])
        picked = jnp.sort(picked)
        return picked + jnp.arange(PAT_DEV, dtype=jnp.int32)
    row_bands = jax.vmap(bands_of_device)(jax.random.split(subkeys[0], device_total))
    row_bands = row_bands.reshape(N_OBJ, N_SUB, N_SCAN, PAT_DEV)
    mirror = jax.random.randint(subkeys[1], (N_OBJ, N_SUB, 1, 1), 0, 2)
    row_bands = jnp.where(mirror == 1, N_SCAN - 2 - row_bands, row_bands)
    shape_full = (N_OBJ, N_SUB, N_SCAN, PAT_DEV)
    row_starts = row_bands * PIX + jax.random.randint(subkeys[2], shape_full, 0, PIX)
    stripe_base = jnp.arange(N_OBJ, dtype=jnp.int32)[:, None, None, None] * TX
    col_starts = stripe_base + jax.random.randint(subkeys[3], shape_full, 0, TX - PIX + 1)
    stacked = jnp.stack([row_starts, col_starts], axis=-1)
    return stacked.reshape(N_OBJ, N_SUB, N_SCAN * PAT_DEV, 2).astype(jnp.int32)


def draw_live_counts(key, part):
    key = jax.random.fold_in(key, 23)
    subkeys = jax.random.split(key, 2)
    lowest = max(1, PAT_DEV - 1)
    counted = jax.random.randint(subkeys[0], (N_OBJ * N_SUB * N_SCAN,), lowest, PAT_DEV + 1)
    chosen = jax.random.randint(subkeys[1], (), 0, N_OBJ * N_SUB * N_SCAN)
    counted = jnp.where(jnp.arange(N_OBJ * N_SUB * N_SCAN) == chosen, PAT_DEV, counted)
    return counted.reshape(N_OBJ, N_SUB, N_SCAN).astype(jnp.int32)


def steps_of(key, shape, pieces, smallest, high):
    def one(position, blocks):
        draws = jax.random.uniform(jax.random.fold_in(jax.random.fold_in(key, 6), position), (blocks,), jnp.float32, smallest / len(pieces), high / len(pieces))
        return jnp.repeat(jnp.exp(draws), shape[position] // blocks).reshape((-1,) + (1,) * (len(shape) - position - 1))

    gain = one(*pieces[0])
    for cut in pieces[1:]:
        gain = gain * one(*cut)
    return gain


def gaussian(rng, dims, scale, limit, shards=(), held_as=jnp.bfloat16):
    array = jax.random.normal(rng, dims, jnp.float32) * scale
    if len(shards) > 0:
        array = steps_of(rng, dims, shards, -0.22, 0.18) * array
    return jnp.clip(array, min=-limit, max=limit).astype(held_as)


def setup_inputs(seed: int = 0, part: int = 0) -> dict:
    splits = jax.random.split(jax.random.key(seed), 6)
    part_splits = jax.random.split(jax.random.fold_in(splits[5], part), 6)
    return {
        "object_field": gaussian(part_splits[0], (2, OBJ_ROWS, OBJ_COLS), 0.5, 3.0, ((1, 16),), jnp.float32),
        "probe_field": gaussian(part_splits[1], (2, PIX, PIX), 0.5, 3.0, (), jnp.float32),
        "intensities": jnp.clip(0.05 + 0.45 * jax.random.uniform(part_splits[2], (N_OBJ, N_SUB, SCANS, PIX, PIX), jnp.float32) ** steps_of(part_splits[2], (N_OBJ, N_SUB, SCANS, PIX, PIX), ((2, 16),), -0.2, 0.2), 0.05, 0.5),
        "positions": draw_positions(jax.random.fold_in(jax.random.fold_in(splits[5], part), 71), part),
        "live_counts": draw_live_counts(jax.random.fold_in(jax.random.fold_in(splits[5], part), 71), part),
    }


def reference(object_field, probe_field, intensities, positions, live_counts):
    rounded = lax.optimization_barrier(object_field.astype(jnp.bfloat16)).astype(jnp.float32)
    probe_complex = probe_field[0] + 1j * probe_field[1]
    flat_measured = intensities.reshape(-1, PIX, PIX)
    flat_places = positions.reshape(-1, 2)
    slot_numbers = jnp.arange(PAT_DEV, dtype=jnp.int32)
    alive = (slot_numbers[None, None, None, :] < live_counts[..., None]).reshape(-1)
    zero_index = jnp.zeros((), jnp.int32)

    def visit(totals, record):
        grad_object, grad_probe = totals
        measured, location, living = record
        start = (zero_index, location[0].astype(jnp.int32), location[1].astype(jnp.int32))
        window = lax.dynamic_slice(rounded, start, (2, PIX, PIX))
        object_complex = window[0] + 1j * window[1]
        exit_wave = probe_complex * object_complex
        far_field = jnp.fft.fft2(exit_wave, norm="ortho")
        power = far_field.real * far_field.real + far_field.imag * far_field.imag
        weighted = (power - measured) * far_field
        back_wave = jnp.fft.ifft2(weighted, norm="ortho") * living.astype(jnp.float32)
        object_step = jnp.conj(probe_complex) * back_wave
        stacked = jnp.stack([object_step.real, object_step.imag])
        stacked = lax.optimization_barrier(stacked.astype(jnp.bfloat16)).astype(jnp.float32)
        probe_term = jnp.conj(object_complex) * back_wave
        grad_probe = grad_probe + jnp.stack([probe_term.real, probe_term.imag])
        current = lax.dynamic_slice(grad_object, start, (2, PIX, PIX))
        grad_object = lax.dynamic_update_slice(grad_object, current + stacked, start)
        return (grad_object, grad_probe), None

    starting = (jnp.zeros((2, OBJ_ROWS, OBJ_COLS), jnp.float32), jnp.zeros((2, PIX, PIX), jnp.float32))
    (object_grad, probe_grad), unused = lax.scan(visit, starting, (flat_measured, flat_places, alive))
    return object_grad, probe_grad
```

```python
import functools
import math

import jax
import jax.numpy as jnp
import numpy as np
from jax import lax
from jax.experimental import pallas as pl
from jax.experimental.pallas import tpu as pltpu
from jax.sharding import PartitionSpec as P

MESH = pl.DeviceIdType.MESH
ANY = pl.BlockSpec(memory_space=pl.ANY)
VMEM = pl.BlockSpec(memory_space=pltpu.VMEM)
ROWS16 = 16


def ring_place(count):
    me = lax.axis_index("scan")
    core = lax.rem(me, 2)
    pair = me // 2
    pos = jnp.where(lax.rem(pair, 2) == 0, pair // 2, count // 2 - 1 - pair // 2)
    return me, core, pos


def pair_at(pos, count):
    pairs = count // 2
    pos = lax.rem(pos + 2 * pairs, pairs)
    return jnp.where(pos < pairs // 2, 2 * pos, 2 * (pairs - 1 - pos) + 1)


def greet(devices):
    barrier = pltpu.get_barrier_semaphore()
    for device in devices:
        pl.semaphore_signal(barrier, inc=1, device_id={"scan": device}, device_id_type=MESH)
    pl.semaphore_wait(barrier, len(devices))


def remote(src, dst, send_sem, recv_sem, device):
    return pltpu.make_async_remote_copy(
        src_ref=src,
        dst_ref=dst,
        send_sem=send_sem,
        recv_sem=recv_sem,
        device_id={"scan": device},
        device_id_type=MESH,
    )


def gather_kernel(count, x_ref, out_ref, zero_ref, zeros, ring_send, ring_recv, pair_send, pair_recv, own_sem, zero_sem):
    me, core, pos = ring_place(count)
    reach = count // 4
    rows = x_ref.shape[1]
    other = me + 1 - 2 * core
    aims = (pair_at(pos + 1, count) * 2 + core, pair_at(pos - 1, count) * 2 + core)
    greet(aims + (other,))

    def slot(distance, which, plane):
        owner = pair_at(pos + distance, count) * 2 + which
        return out_ref.at[plane, pl.ds(pl.multiple_of(owner * rows, rows), rows), :]

    sent = []

    def launch(copy):
        copy.start()
        sent.append(copy)

    def ring_copy(src, way, hop, plane, distance):
        return remote(
            src, slot(distance, core, plane), ring_send.at[way, hop, plane], ring_recv.at[way, hop, plane], aims[way]
        )

    def pair_copy(src, index, plane, distance, which):
        return remote(
            src, slot(distance, which, plane), pair_send.at[index, plane], pair_recv.at[index, plane], other
        )

    for plane in range(2):
        for way in range(2):
            launch(ring_copy(x_ref.at[plane], way, 0, plane, 0))
    for plane in range(2):
        launch(pair_copy(x_ref.at[plane], 0, plane, 0, core))
    own = [pltpu.make_async_copy(x_ref.at[plane], slot(0, core, plane), own_sem.at[plane]) for plane in range(2)]
    for copy in own:
        copy.start()
    zeros[...] = jnp.zeros_like(zeros)
    depth = zeros.shape[1]
    cleared = [
        pltpu.make_async_copy(zeros, zero_ref.at[:, pl.ds(part * depth, depth), :], zero_sem.at[part])
        for part in range(zero_ref.shape[1] // depth)
    ]
    for copy in cleared:
        copy.start()
    for hop in range(reach):
        for plane in range(2):
            for way in range(2):
                if hop == reach - 1 and plane != way:
                    continue
                distance = -(hop + 1) if way == 0 else hop + 1
                here = slot(distance, core, plane)
                ring_copy(here, way, hop, plane, distance).wait_recv()
                if hop < reach - 2 or (hop == reach - 2 and plane == way):
                    launch(ring_copy(here, way, hop + 1, plane, distance))
                index = 1 + 2 * hop + way
                launch(pair_copy(here, index, plane, distance, core))
    for plane in range(2):
        pair_copy(slot(0, 1 - core, plane), 0, plane, 0, 1 - core).wait_recv()
    for hop in range(reach):
        for plane in range(2):
            for way in range(2):
                if hop == reach - 1 and plane != way:
                    continue
                distance = -(hop + 1) if way == 0 else hop + 1
                index = 1 + 2 * hop + way
                pair_copy(slot(distance, 1 - core, plane), index, plane, distance, 1 - core).wait_recv()
    for copy in sent:
        copy.wait_send()
    for copy in own + cleared:
        copy.wait()


def gather_object(tile_low, count):
    planes, rows, columns = tile_low.shape
    whole = jax.ShapeDtypeStruct((planes, count * rows, columns), tile_low.dtype)
    reach = count // 4
    dma = pltpu.SemaphoreType.DMA
    return pl.pallas_call(
        functools.partial(gather_kernel, count),
        out_shape=(whole, whole),
        in_specs=[ANY],
        out_specs=(ANY, ANY),
        scratch_shapes=[
            pltpu.VMEM((planes, 2 * rows, columns), tile_low.dtype),
            dma((2, reach, 2)),
            dma((2, reach, 2)),
            dma((2 * reach + 1, 2)),
            dma((2 * reach + 1, 2)),
            dma((2,)),
            dma((count // 2,)),
        ],
        compiler_params=pltpu.CompilerParams(
            collective_id=0, has_side_effects=True, vmem_limit_bytes=16 * 2**20
        ),
        name="gather_object",
    )(tile_low)


def split(value):
    high = value.astype(jnp.bfloat16)
    return high, (value - high.astype(jnp.float32)).astype(jnp.bfloat16)


def dot(left, right):
    return jnp.dot(left, right, preferred_element_type=jnp.float32)


def product_left(high, low, value):
    first, second = split(value)
    return dot(high[...], first) + (dot(low[...], first) + dot(high[...], second))


def product_right(value, high, low):
    first, second = split(value)
    return dot(first, high[...]) + (dot(first, low[...]) + dot(second, high[...]))


def transform(real_part, imag_part, left, right):
    pixels = real_part.shape[0]
    upright = product_left(*left, jnp.concatenate([real_part, imag_part], axis=0))
    flat = jnp.concatenate([upright[:pixels], upright[pixels:]], axis=1)
    out = product_right(flat, *right)
    return out[:, :pixels], out[:, pixels:]


def pattern_kernel(
    row_ref, col_ref, live_ref, probe_ref, measured_ref, fh_ref, fl_ref, gh_ref, gl_ref, object_ref, blank_ref,
    steps_ref, sum_ref, windows, staged, in_sem, out_sem,
):
    del blank_ref
    slot = pl.program_id(0)
    slots = windows.shape[0]
    pixels = probe_ref.shape[1]
    tall = windows.shape[2]
    stripe = windows.shape[3]

    def aligned(index):
        return pl.multiple_of(row_ref[index] // ROWS16 * ROWS16, ROWS16)

    def fetch(index):
        return pltpu.make_async_copy(
            object_ref.at[:, pl.ds(aligned(index), tall), :], windows.at[index], in_sem.at[index]
        )

    def emit(index):
        return pltpu.make_async_copy(
            staged.at[index], steps_ref.at[:, pl.ds(aligned(index), tall), :], out_sem.at[index]
        )

    @pl.when(slot == 0)
    def _():
        for index in range(slots):
            fetch(index).start()
        sum_ref[...] = jnp.zeros_like(sum_ref)

    fetch(slot).wait()
    row_off = lax.rem(row_ref[slot], ROWS16)
    col = col_ref[slot]
    place = lax.broadcasted_iota(jnp.int32, (stripe, pixels), 0) - lax.broadcasted_iota(
        jnp.int32, (stripe, pixels), 1
    )
    pick = jnp.where(place == col, 1.0, 0.0).astype(jnp.bfloat16)

    def cut(plane):
        moved = dot(windows[slot, plane], pick)
        return pltpu.roll(moved, lax.rem(tall - row_off, tall), 0)[:pixels]

    object_real = cut(0)
    object_imag = cut(1)
    probe_real = probe_ref[0]
    probe_imag = probe_ref[1]
    forward, backward = (fh_ref, fl_ref), (gh_ref, gl_ref)
    far_real, far_imag = transform(
        probe_real * object_real - probe_imag * object_imag,
        probe_real * object_imag + probe_imag * object_real,
        forward,
        backward,
    )
    misfit = far_real * far_real + far_imag * far_imag - measured_ref[0]
    back_real, back_imag = transform(misfit * far_real, misfit * far_imag, backward, forward)
    living = jnp.where(slot < live_ref[0], 1.0, 0.0).astype(jnp.float32)
    back_real = back_real * living
    back_imag = back_imag * living
    sum_ref[0] += object_real * back_real + object_imag * back_imag
    sum_ref[1] += object_real * back_imag - object_imag * back_real

    def put(plane, value):
        low = value.astype(jnp.bfloat16).astype(jnp.float32)
        padded = jnp.concatenate([low, jnp.zeros((tall - pixels, pixels), jnp.float32)], axis=0)
        moved = pltpu.roll(padded, row_off, 0).astype(jnp.bfloat16)
        spread = lax.dot_general(moved, pick, (((1,), (1,)), ((), ())), preferred_element_type=jnp.float32)
        staged[slot, plane] = spread.astype(jnp.bfloat16)

    put(0, probe_real * back_real + probe_imag * back_imag)
    put(1, probe_real * back_imag - probe_imag * back_real)
    emit(slot).start()

    @pl.when(slot == slots - 1)
    def _():
        for index in range(slots):
            emit(index).wait()


def dft_tables(pixels):
    counter = np.arange(pixels)
    angle = (counter[:, None] * counter[None, :] % pixels) * (2.0 * math.pi / pixels)
    cosine = np.cos(angle) / math.sqrt(pixels)
    sine = np.sin(angle) / math.sqrt(pixels)
    tables = []
    for table in (np.block([[cosine, sine], [-sine, cosine]]), np.block([[cosine, -sine], [sine, cosine]])):
        table = table.astype(np.float32)
        high = table.astype(jnp.bfloat16)
        tables += [high, (table - high.astype(np.float32)).astype(jnp.bfloat16)]
    return tables


def pattern_steps(whole, blank, probe_field, measured, rows, cols, live):
    slots, pixels, _ = measured.shape
    stripe = whole.shape[2]
    tall = pixels + ROWS16
    smem = pl.BlockSpec(memory_space=pltpu.SMEM)
    tables = dft_tables(pixels)
    plane = pl.BlockSpec((2, pixels, pixels), lambda slot: (0, 0, 0))
    table = pl.BlockSpec((2 * pixels, 2 * pixels), lambda slot: (0, 0))
    return pl.pallas_call(
        pattern_kernel,
        grid=(slots,),
        out_shape=(
            jax.ShapeDtypeStruct(blank.shape, blank.dtype),
            jax.ShapeDtypeStruct(probe_field.shape, jnp.float32),
        ),
        in_specs=[
            smem, smem, smem, plane, pl.BlockSpec((1, pixels, pixels), lambda slot: (slot, 0, 0)),
            table, table, table, table, ANY, ANY,
        ],
        out_specs=(ANY, plane),
        scratch_shapes=[
            pltpu.VMEM((slots, 2, tall, stripe), jnp.bfloat16),
            pltpu.VMEM((slots, 2, tall, stripe), jnp.bfloat16),
            pltpu.SemaphoreType.DMA((slots,)),
            pltpu.SemaphoreType.DMA((slots,)),
        ],
        input_output_aliases={10: 0},
        compiler_params=pltpu.CompilerParams(vmem_limit_bytes=40 * 2**20),
        name="pattern_steps",
    )(rows, cols, live, probe_field, measured, *tables, whole, blank)


def reduce_kernel(
    count, x_ref, probe_ref, out_ref, probe_out_ref, own, sib, inbox, pown, psib, pinbox, pfinal,
    own_sem, sib_send, sib_recv, ring_send, ring_recv,
    pown_sem, psib_send, psib_recv, pring_send, pring_recv, all_send, all_recv, mate_send, mate_recv, last_sem,
):
    me, core, pos = ring_place(count)
    pairs = count // 2
    reach = pairs // 2
    rows = own.shape[2]
    other = me + 1 - 2 * core
    aims = (pair_at(pos + 1, count) * 2 + core, pair_at(pos - 1, count) * 2 + core)
    greet(aims + (other,))
    sent = []

    def launch(copy):
        copy.start()
        sent.append(copy)

    def band(rel, which, plane):
        owner = pair_at(pos + rel, count) * 2 + which
        return x_ref.at[plane, pl.ds(pl.multiple_of(owner * rows, rows), rows), :]

    def own_copy(rel, plane):
        return pltpu.make_async_copy(band(rel, core, plane), own.at[rel, plane], own_sem.at[rel, plane])

    def sib_copy(rel, plane):
        return remote(
            band(rel, 1 - core, plane), sib.at[rel, plane], sib_send.at[rel, plane], sib_recv.at[rel, plane], other
        )

    def pown_copy(rel):
        return pltpu.make_async_copy(
            probe_ref.at[:, pair_at(pos + rel, count), core], pown.at[rel], pown_sem.at[rel]
        )

    def psib_copy(rel):
        return remote(
            probe_ref.at[:, pair_at(pos + rel, count), 1 - core], psib.at[rel], psib_send.at[rel], psib_recv.at[rel],
            other,
        )

    order = [reach]
    for k in range(reach - 1, 0, -1):
        order += [k, pairs - k]
    order += [0]
    for rel in order[:1]:
        pown_copy(rel).start()
        launch(psib_copy(rel))
        for plane in range(2):
            own_copy(rel, plane).start()
            launch(sib_copy(rel, plane))
    for rel in order[1:]:
        pown_copy(rel).start()
        launch(psib_copy(rel))
    for rel in order[1:]:
        for plane in range(2):
            own_copy(rel, plane).start()
            launch(sib_copy(rel, plane))

    def ring_copy(way, rel, k, plane):
        return remote(
            own.at[rel, plane], inbox.at[way, k - 1, plane], ring_send.at[way, k - 1, plane],
            ring_recv.at[way, k - 1, plane], aims[way],
        )

    def add_rows(target, terms):
        block = 64

        def body(index, carry):
            at = pl.ds(pl.multiple_of(index * block, block), block)
            total = terms[0][at, :].astype(jnp.float32)
            for term in terms[1:]:
                total = total + term[at, :].astype(jnp.float32)
            target[at, :] = total.astype(target.dtype)
            return carry

        lax.fori_loop(0, rows // block, body, 0)

    def main_hop(way, k, plane):
        rel = k if way == 0 else pairs - k
        own_copy(rel, plane).wait()
        sib_copy(rel, plane).wait_recv()
        terms = [own.at[rel, plane], sib.at[rel, plane]]
        if k < reach and not (k == reach - 1 and plane != way):
            ring_copy(way, rel, k + 1, plane).wait_recv()
            terms.append(inbox.at[way, k, plane])
        add_rows(own.at[rel, plane], terms)
        launch(ring_copy(way, rel, k, plane))

    def pring_copy(way, rel, k):
        if k == reach:
            return remote(
                pown.at[rel, way], pinbox.at[way, k - 1, way], pring_send.at[way, k - 1], pring_recv.at[way, k - 1],
                aims[way],
            )
        return remote(
            pown.at[rel], pinbox.at[way, k - 1], pring_send.at[way, k - 1], pring_recv.at[way, k - 1], aims[way]
        )

    def probe_hop(k):
        if k == reach:
            pown_copy(reach).wait()
            psib_copy(reach).wait_recv()
            pown[reach] = pown[reach] + psib[reach]
            for way in range(2):
                launch(pring_copy(way, reach, k))
            return
        for way in range(2):
            rel = k if way == 0 else pairs - k
            pown_copy(rel).wait()
            psib_copy(rel).wait_recv()
            pring_copy(way, rel, k + 1).wait_recv()
            pown[rel] = pown[rel] + psib[rel]
            if k == reach - 1:
                pown[rel, way] = pown[rel, way] + pinbox[way, k, way]
            else:
                pown[rel] = pown[rel] + pinbox[way, k]
            launch(pring_copy(way, rel, k))

    def result(distance, which):
        return probe_out_ref.at[:, pair_at(pos + distance, count), which]

    def all_copy(src, way, hop, distance):
        if hop == reach - 1:
            place = probe_out_ref.at[way, pair_at(pos + distance, count), core]
        else:
            place = result(distance, core)
        return remote(src, place, all_send.at[way, hop], all_recv.at[way, hop], aims[way])

    def mate_copy(src, index, distance, which, plane=None):
        place = result(distance, which)
        if plane is not None:
            place = probe_out_ref.at[plane, pair_at(pos + distance, count), which]
        return remote(src, place, mate_send.at[index], mate_recv.at[index], other)

    last = pltpu.make_async_copy(pfinal, result(0, core), last_sem)

    def probe_finish():
        pown_copy(0).wait()
        psib_copy(0).wait_recv()
        total = pown[0] + psib[0]
        for way in range(2):
            pring_copy(way, 0, 1).wait_recv()
            total = total + pinbox[way, 0]
        pfinal[...] = total
        for way in range(2):
            launch(all_copy(pfinal, way, 0, 0))
        launch(mate_copy(pfinal, 0, 0, core))
        last.start()

    def probe_spread(hop):
        for way in range(2):
            distance = -(hop + 1) if way == 0 else hop + 1
            end = hop == reach - 1
            half = probe_out_ref.at[way, pair_at(pos + distance, count), core]
            here = half if end else result(distance, core)
            all_copy(here, way, hop, distance).wait_recv()
            if not end:
                launch(all_copy(half if hop == reach - 2 else here, way, hop + 1, distance))
            launch(mate_copy(here, 1 + 2 * hop + way, distance, core, way if end else None))

    stages = [functools.partial(probe_hop, k) for k in range(reach, 0, -1)]
    stages += [probe_finish]
    stages += [functools.partial(probe_spread, hop) for hop in range(reach)]
    hops = [[(0, reach, 0), (1, reach, 1)]]
    for k in range(reach - 1, 0, -1):
        for plane in range(2):
            hops.append([(0, k, 1 - plane), (1, k, plane)])
    while stages or hops:
        if stages:
            stages.pop(0)()
        if hops:
            for hop in hops.pop(0):
                main_hop(*hop)

    for plane in range(2):
        own_copy(0, plane).wait()
        sib_copy(0, plane).wait_recv()
        for way in range(2):
            ring_copy(way, 0, 1, plane).wait_recv()
        add_rows(
            out_ref.at[plane], [own.at[0, plane], sib.at[0, plane], inbox.at[0, 0, plane], inbox.at[1, 0, plane]]
        )
    mate_copy(result(0, 1 - core), 0, 0, 1 - core).wait_recv()
    for hop in range(reach):
        for way in range(2):
            distance = -(hop + 1) if way == 0 else hop + 1
            end = hop == reach - 1
            there = probe_out_ref.at[way, pair_at(pos + distance, count), 1 - core] if end else result(distance, 1 - core)
            mate_copy(there, 1 + 2 * hop + way, distance, 1 - core, way if end else None).wait_recv()
    last.wait()
    for copy in sent:
        copy.wait_send()


def reduce_steps(steps, probe_part, count):
    planes, long_rows, columns = steps.shape
    rows = long_rows // count
    pixels = probe_part.shape[1]
    pairs = count // 2
    reach = pairs // 2
    share = pixels // count
    dma = pltpu.SemaphoreType.DMA
    grad, total = pl.pallas_call(
        functools.partial(reduce_kernel, count),
        out_shape=(
            jax.ShapeDtypeStruct((planes, rows, columns), jnp.float32),
            jax.ShapeDtypeStruct((2, pairs, 2, share, pixels), jnp.float32),
        ),
        in_specs=[ANY, ANY],
        out_specs=(VMEM, ANY),
        scratch_shapes=[
            pltpu.VMEM((pairs, 2, rows, columns), jnp.bfloat16),
            pltpu.VMEM((pairs, 2, rows, columns), jnp.bfloat16),
            pltpu.VMEM((2, reach, 2, rows, columns), jnp.bfloat16),
            pltpu.VMEM((pairs, 2, share, pixels), jnp.float32),
            pltpu.VMEM((pairs, 2, share, pixels), jnp.float32),
            pltpu.VMEM((2, reach, 2, share, pixels), jnp.float32),
            pltpu.VMEM((2, share, pixels), jnp.float32),
            dma((pairs, 2)),
            dma((pairs, 2)),
            dma((pairs, 2)),
            dma((2, reach, 2)),
            dma((2, reach, 2)),
            dma((pairs,)),
            dma((pairs,)),
            dma((pairs,)),
            dma((2, reach)),
            dma((2, reach)),
            dma((2, reach)),
            dma((2, reach)),
            dma((2 * reach + 1,)),
            dma((2 * reach + 1,)),
            dma,
        ],
        compiler_params=pltpu.CompilerParams(
            collective_id=1, has_side_effects=True, vmem_limit_bytes=40 * 2**20
        ),
        name="reduce_steps",
    )(steps, probe_part.reshape(2, pairs, 2, share, pixels))
    return grad, total.reshape(2, pixels, pixels)


def on_device(object_field, probe_field, intensities, positions, live_counts):
    pixels = probe_field.shape[1]
    stripe = object_field.shape[2]
    slots = positions.shape[2]
    count = lax.axis_size("scan")
    whole, blank = gather_object(object_field.astype(jnp.bfloat16), count)
    places = positions.reshape(slots, 2)
    steps, probe_part = pattern_steps(
        whole,
        blank,
        probe_field,
        intensities.reshape(slots, pixels, pixels),
        places[:, 0],
        places[:, 1] - lax.axis_index("obj") * stripe,
        live_counts.reshape(1),
    )
    object_grad, probe_grad = reduce_steps(steps, probe_part, count)
    if lax.axis_size("sub") > 1:
        object_grad = lax.psum(object_grad, "sub")
    if lax.axis_size("obj") * lax.axis_size("sub") > 1:
        probe_grad = lax.psum(probe_grad, ("obj", "sub"))
    return (object_grad, probe_grad)


def solution(mesh):
    placed = (
        P(None, ("groups", "scan"), "obj"),
        P("groups", None, None),
        P(("groups", "obj"), "sub", "scan", None, None),
        P(("groups", "obj"), "sub", "scan", None),
        P(("groups", "obj"), "sub", "scan"),
    )
    return jax.shard_map(
        on_device,
        mesh=mesh,
        in_specs=placed,
        out_specs=(P(None, ("groups", "scan"), "obj"), P("groups", None, None)),
        check_vma=False,
    )
```

```python
import functools
import math

import jax
import jax.numpy as jnp
import numpy as np
from jax import lax
from jax.experimental import pallas as pl
from jax.experimental.pallas import tpu as pltpu
from jax.sharding import PartitionSpec as P

MESH = pl.DeviceIdType.MESH
ANY = pl.BlockSpec(memory_space=pl.ANY)
VMEM = pl.BlockSpec(memory_space=pltpu.VMEM)
ROWS16 = 16


def ring_place(count):
    me = lax.axis_index("scan")
    core = lax.rem(me, 2)
    pair = me // 2
    pos = jnp.where(lax.rem(pair, 2) == 0, pair // 2, count // 2 - 1 - pair // 2)
    return me, core, pos


def pair_at(pos, count):
    pairs = count // 2
    pos = lax.rem(pos + 2 * pairs, pairs)
    return jnp.where(pos < pairs // 2, 2 * pos, 2 * (pairs - 1 - pos) + 1)


def greet(devices):
    barrier = pltpu.get_barrier_semaphore()
    for device in devices:
        pl.semaphore_signal(barrier, inc=1, device_id={"scan": device}, device_id_type=MESH)
    pl.semaphore_wait(barrier, len(devices))


def remote(src, dst, send_sem, recv_sem, device):
    return pltpu.make_async_remote_copy(
        src_ref=src,
        dst_ref=dst,
        send_sem=send_sem,
        recv_sem=recv_sem,
        device_id={"scan": device},
        device_id_type=MESH,
    )


def gather_kernel(count, x_ref, out_ref, zero_ref, zeros, ring_send, ring_recv, pair_send, pair_recv, own_sem, zero_sem):
    me, core, pos = ring_place(count)
    reach = count // 4
    rows = x_ref.shape[1]
    other = me + 1 - 2 * core
    aims = (pair_at(pos + 1, count) * 2 + core, pair_at(pos - 1, count) * 2 + core)
    greet(aims + (other,))

    def slot(distance, which, plane):
        owner = pair_at(pos + distance, count) * 2 + which
        return out_ref.at[plane, pl.ds(pl.multiple_of(owner * rows, rows), rows), :]

    sent = []

    def launch(copy):
        copy.start()
        sent.append(copy)

    def ring_copy(src, way, hop, plane, distance):
        return remote(
            src, slot(distance, core, plane), ring_send.at[way, hop, plane], ring_recv.at[way, hop, plane], aims[way]
        )

    def pair_copy(src, index, plane, distance, which):
        return remote(
            src, slot(distance, which, plane), pair_send.at[index, plane], pair_recv.at[index, plane], other
        )

    for plane in range(2):
        for way in range(2):
            launch(ring_copy(x_ref.at[plane], way, 0, plane, 0))
    for plane in range(2):
        launch(pair_copy(x_ref.at[plane], 0, plane, 0, core))
    own = [pltpu.make_async_copy(x_ref.at[plane], slot(0, core, plane), own_sem.at[plane]) for plane in range(2)]
    for copy in own:
        copy.start()
    zeros[...] = jnp.zeros_like(zeros)
    depth = zeros.shape[1]
    cleared = [
        pltpu.make_async_copy(zeros, zero_ref.at[:, pl.ds(part * depth, depth), :], zero_sem.at[part])
        for part in range(zero_ref.shape[1] // depth)
    ]
    for copy in cleared:
        copy.start()
    for hop in range(reach):
        for plane in range(2):
            for way in range(2):
                if hop == reach - 1 and plane != way:
                    continue
                distance = -(hop + 1) if way == 0 else hop + 1
                here = slot(distance, core, plane)
                ring_copy(here, way, hop, plane, distance).wait_recv()
                if hop < reach - 2 or (hop == reach - 2 and plane == way):
                    launch(ring_copy(here, way, hop + 1, plane, distance))
                index = 1 + 2 * hop + way
                launch(pair_copy(here, index, plane, distance, core))
    for plane in range(2):
        pair_copy(slot(0, 1 - core, plane), 0, plane, 0, 1 - core).wait_recv()
    for hop in range(reach):
        for plane in range(2):
            for way in range(2):
                if hop == reach - 1 and plane != way:
                    continue
                distance = -(hop + 1) if way == 0 else hop + 1
                index = 1 + 2 * hop + way
                pair_copy(slot(distance, 1 - core, plane), index, plane, distance, 1 - core).wait_recv()
    for copy in sent:
        copy.wait_send()
    for copy in own + cleared:
        copy.wait()


def gather_object(tile_low, count):
    planes, rows, columns = tile_low.shape
    whole = jax.ShapeDtypeStruct((planes, count * rows, columns), tile_low.dtype)
    reach = count // 4
    dma = pltpu.SemaphoreType.DMA
    return pl.pallas_call(
        functools.partial(gather_kernel, count),
        out_shape=(whole, whole),
        in_specs=[ANY],
        out_specs=(ANY, ANY),
        scratch_shapes=[
            pltpu.VMEM((planes, 2 * rows, columns), tile_low.dtype),
            dma((2, reach, 2)),
            dma((2, reach, 2)),
            dma((2 * reach + 1, 2)),
            dma((2 * reach + 1, 2)),
            dma((2,)),
            dma((count // 2,)),
        ],
        compiler_params=pltpu.CompilerParams(
            collective_id=0, has_side_effects=True, vmem_limit_bytes=16 * 2**20
        ),
        name="gather_object",
    )(tile_low)


def split(value):
    high = value.astype(jnp.bfloat16)
    return high, (value - high.astype(jnp.float32)).astype(jnp.bfloat16)


def product_left(table, value):
    first, second = split(value)
    terms = jnp.concatenate([first, first, second], axis=0)
    return jnp.dot(table[...], terms, preferred_element_type=jnp.float32)


def product_right(value, table):
    first, second = split(value)
    terms = jnp.concatenate([first, first, second], axis=1)
    return jnp.dot(terms, table[...], preferred_element_type=jnp.float32)


def halves(value, axis):
    middle = value.shape[axis] // 2
    if axis == 0:
        return value[:middle], value[middle:]
    return value[:, :middle], value[:, middle:]


def multiply(even, odd, tables, axis):
    found = []
    for table, parts in zip(tables, (even, odd)):
        stacked = jnp.concatenate([jnp.concatenate(part, axis=axis) for part in parts], axis=1 - axis)
        out = product_left(table, stacked) if axis == 0 else product_right(stacked, table)
        size = out.shape[1 - axis] // len(parts)
        planes = [
            out[:, index * size : (index + 1) * size] if axis == 0 else out[index * size : (index + 1) * size]
            for index in range(len(parts))
        ]
        found.append([halves(plane, axis) for plane in planes])
    return found


def ahead(waves, tables, axis):
    even, odd = [], []
    for wave in waves:
        split_parts = [halves(part, axis) for part in wave]
        even.append([first + second for first, second in split_parts])
        odd.append([first - second for first, second in split_parts])
    found = multiply(even, odd, tables, axis)
    return [
        tuple(jnp.concatenate([one, two], axis=axis) for one, two in zip(low, high)) for low, high in zip(*found)
    ]


def behind(waves, tables, axis):
    even = [[halves(part, axis)[0] for part in wave] for wave in waves]
    odd = [[halves(part, axis)[1] for part in wave] for wave in waves]
    found = multiply(even, odd, tables, axis)
    return [
        tuple(jnp.concatenate([one + two, one - two], axis=axis) for one, two in zip(low, high))
        for low, high in zip(*found)
    ]


def reorder(value, down, across):
    size = value.shape[0]
    first, second = split(value)
    both = jnp.dot(jnp.concatenate([first, second], axis=0), across, preferred_element_type=jnp.float32)
    both = both.astype(jnp.bfloat16)
    both = jnp.concatenate([both[:size], both[size:]], axis=1)
    both = jnp.dot(down, both, preferred_element_type=jnp.float32)
    return both[:, :size] + both[:, size:]


GROUP = 3


def pattern_kernel(
    row_ref, col_ref, live_ref, probe_ref, measured_ref, down_ref, across_ref, *rest,
):
    tables, rest = rest[:8], rest[8:]
    (object_ref, blank_ref, steps_ref, sum_ref, windows, staged, in_sem, out_sem) = rest
    del blank_ref
    turn = pl.program_id(0)
    slots = windows.shape[0]
    group = measured_ref.shape[0]
    pixels = probe_ref.shape[1]
    tall = windows.shape[2]
    stripe = windows.shape[3]

    def aligned(index):
        return pl.multiple_of(row_ref[index] // ROWS16 * ROWS16, ROWS16)

    def fetch(index):
        return pltpu.make_async_copy(
            object_ref.at[:, pl.ds(aligned(index), tall), :], windows.at[index], in_sem.at[index]
        )

    def emit(index):
        return pltpu.make_async_copy(
            staged.at[index], steps_ref.at[:, pl.ds(aligned(index), tall), :], out_sem.at[index]
        )

    @pl.when(turn == 0)
    def _():
        for index in range(slots):
            fetch(index).start()
        sum_ref[...] = jnp.zeros_like(sum_ref)

    for member in range(group):
        fetch(turn * group + member).wait()
    apart = lax.broadcasted_iota(jnp.int32, (stripe, pixels), 0) - lax.broadcasted_iota(
        jnp.int32, (stripe, pixels), 1
    )
    picks, patches, waves = [], [], []
    probe_real = probe_ref[0]
    probe_imag = probe_ref[1]
    for member in range(group):
        slot = turn * group + member
        pick = jnp.where(apart == col_ref[slot], 1.0, 0.0).astype(jnp.bfloat16)
        both = jnp.concatenate([windows[slot, 0], windows[slot, 1]], axis=0)
        moved = jnp.dot(both, pick, preferred_element_type=jnp.float32)
        shift = lax.rem(tall - lax.rem(row_ref[slot], ROWS16), tall)
        object_real = pltpu.roll(moved[:tall], shift, 0)[:pixels]
        object_imag = pltpu.roll(moved[tall:], shift, 0)[:pixels]
        picks.append(pick)
        patches.append((object_real, object_imag))
        waves.append(
            (
                probe_real * object_real - probe_imag * object_imag,
                probe_real * object_imag + probe_imag * object_real,
            )
        )
    far = ahead(ahead(waves, tables[0:2], 0), tables[2:4], 1)
    weighted = []
    for member in range(group):
        far_real, far_imag = far[member]
        misfit = far_real * far_real + far_imag * far_imag - reorder(
            measured_ref[member], down_ref[...], across_ref[...]
        )
        weighted.append((misfit * far_real, misfit * far_imag))
    back = behind(behind(weighted, tables[4:6], 0), tables[6:8], 1)
    total_real, total_imag = sum_ref[0], sum_ref[1]
    for member in range(group):
        slot = turn * group + member
        living = jnp.where(slot < live_ref[0], 1.0, 0.0).astype(jnp.float32)
        back_real, back_imag = back[member][0] * living, back[member][1] * living
        object_real, object_imag = patches[member]
        total_real += object_real * back_real + object_imag * back_imag
        total_imag += object_real * back_imag - object_imag * back_real
        row_off = lax.rem(row_ref[slot], ROWS16)

        def shifted(value):
            low = value.astype(jnp.bfloat16).astype(jnp.float32)
            padded = jnp.concatenate([low, jnp.zeros((tall - pixels, pixels), jnp.float32)], axis=0)
            return pltpu.roll(padded, row_off, 0).astype(jnp.bfloat16)

        both = jnp.concatenate(
            [
                shifted(probe_real * back_real + probe_imag * back_imag),
                shifted(probe_real * back_imag - probe_imag * back_real),
            ],
            axis=0,
        )
        spread = lax.dot_general(both, picks[member], (((1,), (1,)), ((), ())), preferred_element_type=jnp.float32)
        spread = spread.astype(jnp.bfloat16)
        staged[slot, 0] = spread[:tall]
        staged[slot, 1] = spread[tall:]
        emit(slot).start()
    sum_ref[0] = total_real
    sum_ref[1] = total_imag

    @pl.when(turn == slots // group - 1)
    def _():
        for index in range(slots):
            emit(index).wait()


def dft_tables(pixels):
    half = pixels // 2
    order = np.concatenate([np.arange(0, pixels, 2), np.arange(1, pixels, 2)])
    down = np.eye(pixels, dtype=np.float32)[order]
    tables = [down.astype(jnp.bfloat16), np.ascontiguousarray(down.T).astype(jnp.bfloat16)]
    point = np.arange(half)
    kinds = []
    for odd in range(2):
        turns = (2 * point[:, None] + odd) * point[None, :] % pixels
        kinds.append(np.exp(-2j * math.pi * turns / pixels) / math.sqrt(pixels))
    for place in (lambda kind: kind, lambda kind: kind.T, lambda kind: kind.conj().T, lambda kind: kind.conj()):
        axis = (len(tables) // 2 + 1) % 2
        for kind in kinds:
            kind = place(kind)
            sign = 1 if axis else -1
            table = np.block([[kind.real, sign * kind.imag], [-sign * kind.imag, kind.real]]).astype(np.float32)
            high = table.astype(jnp.bfloat16)
            low = (table - high.astype(np.float32)).astype(jnp.bfloat16)
            tables.append(np.concatenate([high, low, high], axis=1 - axis))
    return tables


def pattern_steps(whole, blank, probe_field, measured, rows, cols, live):
    slots, pixels, _ = measured.shape
    stripe = whole.shape[2]
    tall = pixels + ROWS16
    group = GROUP if slots % GROUP == 0 else 1
    smem = pl.BlockSpec(memory_space=pltpu.SMEM)
    tables = dft_tables(pixels)
    plane = pl.BlockSpec((2, pixels, pixels), lambda turn: (0, 0, 0))
    return pl.pallas_call(
        pattern_kernel,
        grid=(slots // group,),
        out_shape=(
            jax.ShapeDtypeStruct(blank.shape, blank.dtype),
            jax.ShapeDtypeStruct(probe_field.shape, jnp.float32),
        ),
        in_specs=[
            smem, smem, smem, plane, pl.BlockSpec((group, pixels, pixels), lambda turn: (turn, 0, 0)),
            *[pl.BlockSpec(table.shape, lambda turn: (0, 0)) for table in tables], ANY, ANY,
        ],
        out_specs=(ANY, plane),
        scratch_shapes=[
            pltpu.VMEM((slots, 2, tall, stripe), jnp.bfloat16),
            pltpu.VMEM((slots, 2, tall, stripe), jnp.bfloat16),
            pltpu.SemaphoreType.DMA((slots,)),
            pltpu.SemaphoreType.DMA((slots,)),
        ],
        input_output_aliases={6 + len(tables): 0},
        compiler_params=pltpu.CompilerParams(vmem_limit_bytes=60 * 2**20),
        name="pattern_steps",
    )(rows, cols, live, probe_field, measured, *tables, whole, blank)


def reduce_kernel(
    count, x_ref, probe_ref, out_ref, probe_out_ref, own, sib, inbox, pown, psib, pinbox, pfinal,
    own_sem, sib_send, sib_recv, ring_send, ring_recv,
    pown_sem, psib_send, psib_recv, pring_send, pring_recv, all_send, all_recv, mate_send, mate_recv, last_sem,
):
    me, core, pos = ring_place(count)
    pairs = count // 2
    reach = pairs // 2
    rows = own.shape[2]
    other = me + 1 - 2 * core
    aims = (pair_at(pos + 1, count) * 2 + core, pair_at(pos - 1, count) * 2 + core)
    greet(aims + (other,))
    sent = []

    def launch(copy):
        copy.start()
        sent.append(copy)

    def band(rel, which, plane):
        owner = pair_at(pos + rel, count) * 2 + which
        return x_ref.at[plane, pl.ds(pl.multiple_of(owner * rows, rows), rows), :]

    def own_copy(rel, plane):
        return pltpu.make_async_copy(band(rel, core, plane), own.at[rel, plane], own_sem.at[rel, plane])

    def sib_copy(rel, plane):
        return remote(
            band(rel, 1 - core, plane), sib.at[rel, plane], sib_send.at[rel, plane], sib_recv.at[rel, plane], other
        )

    def pown_copy(rel):
        return pltpu.make_async_copy(
            probe_ref.at[:, pair_at(pos + rel, count), core], pown.at[rel], pown_sem.at[rel]
        )

    def psib_copy(rel):
        return remote(
            probe_ref.at[:, pair_at(pos + rel, count), 1 - core], psib.at[rel], psib_send.at[rel], psib_recv.at[rel],
            other,
        )

    order = [reach]
    for k in range(reach - 1, 0, -1):
        order += [k, pairs - k]
    order += [0]
    for rel in order[:1]:
        pown_copy(rel).start()
        launch(psib_copy(rel))
        for plane in range(2):
            own_copy(rel, plane).start()
            launch(sib_copy(rel, plane))
    for rel in order[1:]:
        pown_copy(rel).start()
        launch(psib_copy(rel))
    for rel in order[1:]:
        for plane in range(2):
            own_copy(rel, plane).start()
            launch(sib_copy(rel, plane))

    def ring_copy(way, rel, k, plane):
        return remote(
            own.at[rel, plane], inbox.at[way, k - 1, plane], ring_send.at[way, k - 1, plane],
            ring_recv.at[way, k - 1, plane], aims[way],
        )

    def add_rows(target, terms):
        block = 64

        def body(index, carry):
            at = pl.ds(pl.multiple_of(index * block, block), block)
            total = terms[0][at, :].astype(jnp.float32)
            for term in terms[1:]:
                total = total + term[at, :].astype(jnp.float32)
            target[at, :] = total.astype(target.dtype)
            return carry

        lax.fori_loop(0, rows // block, body, 0)

    def main_hop(way, k, plane):
        rel = k if way == 0 else pairs - k
        own_copy(rel, plane).wait()
        sib_copy(rel, plane).wait_recv()
        terms = [own.at[rel, plane], sib.at[rel, plane]]
        if k < reach and not (k == reach - 1 and plane != way):
            ring_copy(way, rel, k + 1, plane).wait_recv()
            terms.append(inbox.at[way, k, plane])
        add_rows(own.at[rel, plane], terms)
        launch(ring_copy(way, rel, k, plane))

    def pring_copy(way, rel, k):
        if k == reach:
            return remote(
                pown.at[rel, way], pinbox.at[way, k - 1, way], pring_send.at[way, k - 1], pring_recv.at[way, k - 1],
                aims[way],
            )
        return remote(
            pown.at[rel], pinbox.at[way, k - 1], pring_send.at[way, k - 1], pring_recv.at[way, k - 1], aims[way]
        )

    def probe_hop(k):
        if k == reach:
            pown_copy(reach).wait()
            psib_copy(reach).wait_recv()
            pown[reach] = pown[reach] + psib[reach]
            for way in range(2):
                launch(pring_copy(way, reach, k))
            return
        for way in range(2):
            rel = k if way == 0 else pairs - k
            pown_copy(rel).wait()
            psib_copy(rel).wait_recv()
            pring_copy(way, rel, k + 1).wait_recv()
            pown[rel] = pown[rel] + psib[rel]
            if k == reach - 1:
                pown[rel, way] = pown[rel, way] + pinbox[way, k, way]
            else:
                pown[rel] = pown[rel] + pinbox[way, k]
            launch(pring_copy(way, rel, k))

    def result(distance, which):
        return probe_out_ref.at[:, pair_at(pos + distance, count), which]

    def all_copy(src, way, hop, distance):
        if hop == reach - 1:
            place = probe_out_ref.at[way, pair_at(pos + distance, count), core]
        else:
            place = result(distance, core)
        return remote(src, place, all_send.at[way, hop], all_recv.at[way, hop], aims[way])

    def mate_copy(src, index, distance, which, plane=None):
        place = result(distance, which)
        if plane is not None:
            place = probe_out_ref.at[plane, pair_at(pos + distance, count), which]
        return remote(src, place, mate_send.at[index], mate_recv.at[index], other)

    last = pltpu.make_async_copy(pfinal, result(0, core), last_sem)

    def probe_finish():
        pown_copy(0).wait()
        psib_copy(0).wait_recv()
        total = pown[0] + psib[0]
        for way in range(2):
            pring_copy(way, 0, 1).wait_recv()
            total = total + pinbox[way, 0]
        pfinal[...] = total
        for way in range(2):
            launch(all_copy(pfinal, way, 0, 0))
        launch(mate_copy(pfinal, 0, 0, core))
        last.start()

    def probe_spread(hop):
        for way in range(2):
            distance = -(hop + 1) if way == 0 else hop + 1
            end = hop == reach - 1
            half = probe_out_ref.at[way, pair_at(pos + distance, count), core]
            here = half if end else result(distance, core)
            all_copy(here, way, hop, distance).wait_recv()
            if not end:
                launch(all_copy(half if hop == reach - 2 else here, way, hop + 1, distance))
            launch(mate_copy(here, 1 + 2 * hop + way, distance, core, way if end else None))

    stages = [functools.partial(probe_hop, k) for k in range(reach, 0, -1)]
    stages += [probe_finish]
    stages += [functools.partial(probe_spread, hop) for hop in range(reach)]
    hops = [[(0, reach, 0), (1, reach, 1)]]
    for k in range(reach - 1, 0, -1):
        for plane in range(2):
            hops.append([(0, k, 1 - plane), (1, k, plane)])
    while stages or hops:
        if stages:
            stages.pop(0)()
        if hops:
            for hop in hops.pop(0):
                main_hop(*hop)

    for plane in range(2):
        own_copy(0, plane).wait()
        sib_copy(0, plane).wait_recv()
        for way in range(2):
            ring_copy(way, 0, 1, plane).wait_recv()
        add_rows(
            out_ref.at[plane], [own.at[0, plane], sib.at[0, plane], inbox.at[0, 0, plane], inbox.at[1, 0, plane]]
        )
    mate_copy(result(0, 1 - core), 0, 0, 1 - core).wait_recv()
    for hop in range(reach):
        for way in range(2):
            distance = -(hop + 1) if way == 0 else hop + 1
            end = hop == reach - 1
            there = probe_out_ref.at[way, pair_at(pos + distance, count), 1 - core] if end else result(distance, 1 - core)
            mate_copy(there, 1 + 2 * hop + way, distance, 1 - core, way if end else None).wait_recv()
    last.wait()
    for copy in sent:
        copy.wait_send()


def reduce_steps(steps, probe_part, count):
    planes, long_rows, columns = steps.shape
    rows = long_rows // count
    pixels = probe_part.shape[1]
    pairs = count // 2
    reach = pairs // 2
    share = pixels // count
    dma = pltpu.SemaphoreType.DMA
    grad, total = pl.pallas_call(
        functools.partial(reduce_kernel, count),
        out_shape=(
            jax.ShapeDtypeStruct((planes, rows, columns), jnp.float32),
            jax.ShapeDtypeStruct((2, pairs, 2, share, pixels), jnp.float32),
        ),
        in_specs=[ANY, ANY],
        out_specs=(VMEM, ANY),
        scratch_shapes=[
            pltpu.VMEM((pairs, 2, rows, columns), jnp.bfloat16),
            pltpu.VMEM((pairs, 2, rows, columns), jnp.bfloat16),
            pltpu.VMEM((2, reach, 2, rows, columns), jnp.bfloat16),
            pltpu.VMEM((pairs, 2, share, pixels), jnp.float32),
            pltpu.VMEM((pairs, 2, share, pixels), jnp.float32),
            pltpu.VMEM((2, reach, 2, share, pixels), jnp.float32),
            pltpu.VMEM((2, share, pixels), jnp.float32),
            dma((pairs, 2)),
            dma((pairs, 2)),
            dma((pairs, 2)),
            dma((2, reach, 2)),
            dma((2, reach, 2)),
            dma((pairs,)),
            dma((pairs,)),
            dma((pairs,)),
            dma((2, reach)),
            dma((2, reach)),
            dma((2, reach)),
            dma((2, reach)),
            dma((2 * reach + 1,)),
            dma((2 * reach + 1,)),
            dma,
        ],
        compiler_params=pltpu.CompilerParams(
            collective_id=1, has_side_effects=True, vmem_limit_bytes=40 * 2**20
        ),
        name="reduce_steps",
    )(steps, probe_part.reshape(2, pairs, 2, share, pixels))
    return grad, total.reshape(2, pixels, pixels)


def on_device(object_field, probe_field, intensities, positions, live_counts):
    pixels = probe_field.shape[1]
    stripe = object_field.shape[2]
    slots = positions.shape[2]
    count = lax.axis_size("scan")
    whole, blank = gather_object(object_field.astype(jnp.bfloat16), count)
    places = positions.reshape(slots, 2)
    steps, probe_part = pattern_steps(
        whole,
        blank,
        probe_field,
        intensities.reshape(slots, pixels, pixels),
        places[:, 0],
        places[:, 1] - lax.axis_index("obj") * stripe,
        live_counts.reshape(1),
    )
    object_grad, probe_grad = reduce_steps(steps, probe_part, count)
    if lax.axis_size("sub") > 1:
        object_grad = lax.psum(object_grad, "sub")
    if lax.axis_size("obj") * lax.axis_size("sub") > 1:
        probe_grad = lax.psum(probe_grad, ("obj", "sub"))
    return (object_grad, probe_grad)


def solution(mesh):
    placed = (
        P(None, ("groups", "scan"), "obj"),
        P("groups", None, None),
        P(("groups", "obj"), "sub", "scan", None, None),
        P(("groups", "obj"), "sub", "scan", None),
        P(("groups", "obj"), "sub", "scan"),
    )
    return jax.shard_map(
        on_device,
        mesh=mesh,
        in_specs=placed,
        out_specs=(P(None, ("groups", "scan"), "obj"), P("groups", None, None)),
        check_vma=False,
    )
```

```python
import functools
import math

import jax
import jax.numpy as jnp
import numpy as np
from jax import lax
from jax.experimental import pallas as pl
from jax.experimental.pallas import tpu as pltpu
from jax.sharding import PartitionSpec as P

MESH = pl.DeviceIdType.MESH
ANY = pl.BlockSpec(memory_space=pl.ANY)
HBM = pl.BlockSpec(memory_space=pltpu.HBM)
VMEM = pl.BlockSpec(memory_space=pltpu.VMEM)
ROWS16 = 16


def ring_place(count):
    me = lax.axis_index("scan")
    core = lax.rem(me, 2)
    pair = me // 2
    pos = jnp.where(lax.rem(pair, 2) == 0, pair // 2, count // 2 - 1 - pair // 2)
    return me, core, pos


def pair_at(pos, count):
    pairs = count // 2
    pos = lax.rem(pos + 2 * pairs, pairs)
    return jnp.where(pos < pairs // 2, 2 * pos, 2 * (pairs - 1 - pos) + 1)


def greet(devices):
    barrier = pltpu.get_barrier_semaphore()
    for device in devices:
        pl.semaphore_signal(barrier, inc=1, device_id={"scan": device}, device_id_type=MESH)
    pl.semaphore_wait(barrier, len(devices))


def remote(src, dst, send_sem, recv_sem, device):
    return pltpu.make_async_remote_copy(
        src_ref=src,
        dst_ref=dst,
        send_sem=send_sem,
        recv_sem=recv_sem,
        device_id={"scan": device},
        device_id_type=MESH,
    )


def gather_kernel(count, x_ref, out_ref, zero_ref, zeros, ring_send, ring_recv, pair_send, pair_recv, own_sem, zero_sem):
    me, core, pos = ring_place(count)
    reach = count // 4
    rows = x_ref.shape[1]
    other = me + 1 - 2 * core
    aims = (pair_at(pos + 1, count) * 2 + core, pair_at(pos - 1, count) * 2 + core)
    greet(aims + (other,))

    def slot(distance, which, plane):
        owner = pair_at(pos + distance, count) * 2 + which
        return out_ref.at[plane, pl.ds(pl.multiple_of(owner * rows, rows), rows), :]

    sent = []

    def launch(copy):
        copy.start()
        sent.append(copy)

    def ring_copy(src, way, hop, plane, distance):
        return remote(
            src, slot(distance, core, plane), ring_send.at[way, hop, plane], ring_recv.at[way, hop, plane], aims[way]
        )

    def pair_copy(src, index, plane, distance, which):
        return remote(
            src, slot(distance, which, plane), pair_send.at[index, plane], pair_recv.at[index, plane], other
        )

    for plane in range(2):
        for way in range(2):
            launch(ring_copy(x_ref.at[plane], way, 0, plane, 0))
    for plane in range(2):
        launch(pair_copy(x_ref.at[plane], 0, plane, 0, core))
    own = [pltpu.make_async_copy(x_ref.at[plane], slot(0, core, plane), own_sem.at[plane]) for plane in range(2)]
    for copy in own:
        copy.start()
    zeros[...] = jnp.zeros_like(zeros)
    depth = zeros.shape[1]
    cleared = [
        pltpu.make_async_copy(zeros, zero_ref.at[:, pl.ds(part * depth, depth), :], zero_sem.at[part])
        for part in range(zero_ref.shape[1] // depth)
    ]
    for copy in cleared:
        copy.start()
    for hop in range(reach):
        for plane in range(2):
            for way in range(2):
                if hop == reach - 1 and plane != way:
                    continue
                distance = -(hop + 1) if way == 0 else hop + 1
                here = slot(distance, core, plane)
                ring_copy(here, way, hop, plane, distance).wait_recv()
                if hop < reach - 2 or (hop == reach - 2 and plane == way):
                    launch(ring_copy(here, way, hop + 1, plane, distance))
                index = 1 + 2 * hop + way
                launch(pair_copy(here, index, plane, distance, core))
    for plane in range(2):
        pair_copy(slot(0, 1 - core, plane), 0, plane, 0, 1 - core).wait_recv()
    for hop in range(reach):
        for plane in range(2):
            for way in range(2):
                if hop == reach - 1 and plane != way:
                    continue
                distance = -(hop + 1) if way == 0 else hop + 1
                index = 1 + 2 * hop + way
                pair_copy(slot(distance, 1 - core, plane), index, plane, distance, 1 - core).wait_recv()
    for copy in sent:
        copy.wait_send()
    for copy in own + cleared:
        copy.wait()


def gather_object(tile_low, count):
    planes, rows, columns = tile_low.shape
    whole = jax.ShapeDtypeStruct((planes, count * rows, columns), tile_low.dtype)
    reach = count // 4
    dma = pltpu.SemaphoreType.DMA
    return pl.pallas_call(
        functools.partial(gather_kernel, count),
        out_shape=(whole, whole),
        in_specs=[ANY],
        out_specs=(HBM, HBM),
        scratch_shapes=[
            pltpu.VMEM((planes, 2 * rows, columns), tile_low.dtype),
            dma((2, reach, 2)),
            dma((2, reach, 2)),
            dma((2 * reach + 1, 2)),
            dma((2 * reach + 1, 2)),
            dma((2,)),
            dma((count // 2,)),
        ],
        compiler_params=pltpu.CompilerParams(
            collective_id=0, has_side_effects=True, vmem_limit_bytes=60 * 2**20
        ),
        name="gather_object",
    )(tile_low)


def split(value):
    high = value.astype(jnp.bfloat16)
    return high, (value - high.astype(jnp.float32)).astype(jnp.bfloat16)


def product_left(table, value):
    first, second = split(value)
    terms = jnp.concatenate([first, first, second], axis=0)
    return jnp.dot(table[...], terms, preferred_element_type=jnp.float32)


def product_right(value, table):
    first, second = split(value)
    terms = jnp.concatenate([first, first, second], axis=1)
    return jnp.dot(terms, table[...], preferred_element_type=jnp.float32)


def halves(value, axis):
    middle = value.shape[axis] // 2
    if axis == 0:
        return value[:middle], value[middle:]
    return value[:, :middle], value[:, middle:]


def multiply(even, odd, tables, axis):
    found = []
    for table, parts in zip(tables, (even, odd)):
        stacked = jnp.concatenate([jnp.concatenate(part, axis=axis) for part in parts], axis=1 - axis)
        out = product_left(table, stacked) if axis == 0 else product_right(stacked, table)
        size = out.shape[1 - axis] // len(parts)
        planes = [
            out[:, index * size : (index + 1) * size] if axis == 0 else out[index * size : (index + 1) * size]
            for index in range(len(parts))
        ]
        found.append([halves(plane, axis) for plane in planes])
    return found


def ahead(waves, tables, axis):
    even, odd = [], []
    for wave in waves:
        split_parts = [halves(part, axis) for part in wave]
        even.append([first + second for first, second in split_parts])
        odd.append([first - second for first, second in split_parts])
    found = multiply(even, odd, tables, axis)
    return [
        tuple(jnp.concatenate([one, two], axis=axis) for one, two in zip(low, high)) for low, high in zip(*found)
    ]


def behind(waves, tables, axis):
    even = [[halves(part, axis)[0] for part in wave] for wave in waves]
    odd = [[halves(part, axis)[1] for part in wave] for wave in waves]
    found = multiply(even, odd, tables, axis)
    return [
        tuple(jnp.concatenate([one + two, one - two], axis=axis) for one, two in zip(low, high))
        for low, high in zip(*found)
    ]


def reorder(value, down, across):
    size = value.shape[0]
    first, second = split(value)
    both = jnp.dot(jnp.concatenate([first, second], axis=0), across, preferred_element_type=jnp.float32)
    both = both.astype(jnp.bfloat16)
    both = jnp.concatenate([both[:size], both[size:]], axis=1)
    both = jnp.dot(down, both, preferred_element_type=jnp.float32)
    return both[:, :size] + both[:, size:]


GROUP = 3


def pattern_kernel(
    place_ref, live_ref, probe_ref, measured_ref, down_ref, across_ref, *rest,
):
    tables, rest = rest[:8], rest[8:]
    (object_ref, blank_ref, steps_ref, sum_ref, windows, staged, in_sem, out_sem) = rest
    del blank_ref
    turn = pl.program_id(0)
    slots = windows.shape[0]
    group = measured_ref.shape[0]
    pixels = probe_ref.shape[1]
    tall = windows.shape[2]
    stripe = windows.shape[3]

    def aligned(index):
        return pl.multiple_of(place_ref[index, 0] // ROWS16 * ROWS16, ROWS16)

    def fetch(index):
        return pltpu.make_async_copy(
            object_ref.at[:, pl.ds(aligned(index), tall), :], windows.at[index], in_sem.at[index]
        )

    def emit(index):
        return pltpu.make_async_copy(
            staged.at[index], steps_ref.at[:, pl.ds(aligned(index), tall), :], out_sem.at[index]
        )

    @pl.when(turn == 0)
    def _():
        for index in range(slots):
            fetch(index).start()
        sum_ref[...] = jnp.zeros_like(sum_ref)

    for member in range(group):
        fetch(turn * group + member).wait()
    apart = lax.broadcasted_iota(jnp.int32, (stripe, pixels), 0) - lax.broadcasted_iota(
        jnp.int32, (stripe, pixels), 1
    )
    column_base = lax.axis_index("obj") * stripe
    picks, patches, waves = [], [], []
    probe_real = probe_ref[0]
    probe_imag = probe_ref[1]
    for member in range(group):
        slot = turn * group + member
        pick = jnp.where(apart == place_ref[slot, 1] - column_base, 1.0, 0.0).astype(jnp.bfloat16)
        both = jnp.concatenate([windows[slot, 0], windows[slot, 1]], axis=0)
        moved = jnp.dot(both, pick, preferred_element_type=jnp.float32)
        shift = lax.rem(tall - lax.rem(place_ref[slot, 0], ROWS16), tall)
        object_real = pltpu.roll(moved[:tall], shift, 0)[:pixels]
        object_imag = pltpu.roll(moved[tall:], shift, 0)[:pixels]
        picks.append(pick)
        patches.append((object_real, object_imag))
        waves.append(
            (
                probe_real * object_real - probe_imag * object_imag,
                probe_real * object_imag + probe_imag * object_real,
            )
        )
    far = ahead(ahead(waves, tables[0:2], 0), tables[2:4], 1)
    weighted = []
    for member in range(group):
        far_real, far_imag = far[member]
        misfit = far_real * far_real + far_imag * far_imag - reorder(
            measured_ref[member], down_ref[...], across_ref[...]
        )
        weighted.append((misfit * far_real, misfit * far_imag))
    back = behind(behind(weighted, tables[4:6], 0), tables[6:8], 1)
    total_real, total_imag = sum_ref[0], sum_ref[1]
    for member in range(group):
        slot = turn * group + member
        living = jnp.where(slot < live_ref[0], 1.0, 0.0).astype(jnp.float32)
        back_real, back_imag = back[member][0] * living, back[member][1] * living
        object_real, object_imag = patches[member]
        total_real += object_real * back_real + object_imag * back_imag
        total_imag += object_real * back_imag - object_imag * back_real
        row_off = lax.rem(place_ref[slot, 0], ROWS16)

        def shifted(value):
            low = value.astype(jnp.bfloat16).astype(jnp.float32)
            padded = jnp.concatenate([low, jnp.zeros((tall - pixels, pixels), jnp.float32)], axis=0)
            return pltpu.roll(padded, row_off, 0).astype(jnp.bfloat16)

        both = jnp.concatenate(
            [
                shifted(probe_real * back_real + probe_imag * back_imag),
                shifted(probe_real * back_imag - probe_imag * back_real),
            ],
            axis=0,
        )
        spread = lax.dot_general(both, picks[member], (((1,), (1,)), ((), ())), preferred_element_type=jnp.float32)
        spread = spread.astype(jnp.bfloat16)
        staged[slot, 0] = spread[:tall]
        staged[slot, 1] = spread[tall:]
        emit(slot).start()
    sum_ref[0] = total_real
    sum_ref[1] = total_imag

    @pl.when(turn == slots // group - 1)
    def _():
        for index in range(slots):
            emit(index).wait()


def dft_tables(pixels):
    half = pixels // 2
    order = np.concatenate([np.arange(0, pixels, 2), np.arange(1, pixels, 2)])
    down = np.eye(pixels, dtype=np.float32)[order]
    tables = [down.astype(jnp.bfloat16), np.ascontiguousarray(down.T).astype(jnp.bfloat16)]
    point = np.arange(half)
    kinds = []
    for odd in range(2):
        turns = (2 * point[:, None] + odd) * point[None, :] % pixels
        kinds.append(np.exp(-2j * math.pi * turns / pixels) / math.sqrt(pixels))
    for place in (lambda kind: kind, lambda kind: kind.T, lambda kind: kind.conj().T, lambda kind: kind.conj()):
        axis = (len(tables) // 2 + 1) % 2
        for kind in kinds:
            kind = place(kind)
            sign = 1 if axis else -1
            table = np.block([[kind.real, sign * kind.imag], [-sign * kind.imag, kind.real]]).astype(np.float32)
            high = table.astype(jnp.bfloat16)
            low = (table - high.astype(np.float32)).astype(jnp.bfloat16)
            tables.append(np.concatenate([high, low, high], axis=1 - axis))
    return tables


def pattern_steps(whole, blank, probe_field, measured, places, live):
    slots, pixels, _ = measured.shape
    stripe = whole.shape[2]
    tall = pixels + ROWS16
    group = GROUP if slots % GROUP == 0 else 1
    smem = pl.BlockSpec(memory_space=pltpu.SMEM)
    tables = dft_tables(pixels)
    plane = pl.BlockSpec((2, pixels, pixels), lambda turn: (0, 0, 0))
    return pl.pallas_call(
        pattern_kernel,
        grid=(slots // group,),
        out_shape=(
            jax.ShapeDtypeStruct(blank.shape, blank.dtype),
            jax.ShapeDtypeStruct(probe_field.shape, jnp.float32),
        ),
        in_specs=[
            smem, smem, plane, pl.BlockSpec((group, pixels, pixels), lambda turn: (turn, 0, 0)),
            *[pl.BlockSpec(table.shape, lambda turn: (0, 0)) for table in tables], HBM, HBM,
        ],
        out_specs=(HBM, plane),
        scratch_shapes=[
            pltpu.VMEM((slots, 2, tall, stripe), jnp.bfloat16),
            pltpu.VMEM((slots, 2, tall, stripe), jnp.bfloat16),
            pltpu.SemaphoreType.DMA((slots,)),
            pltpu.SemaphoreType.DMA((slots,)),
        ],
        input_output_aliases={5 + len(tables): 0},
        compiler_params=pltpu.CompilerParams(vmem_limit_bytes=60 * 2**20),
        name="pattern_steps",
    )(places, live, probe_field, measured, *tables, whole, blank)


def reduce_kernel(
    count, x_ref, probe_ref, out_ref, probe_out_ref, own, sib, inbox, pown, psib, pinbox, pfinal,
    own_sem, sib_send, sib_recv, ring_send, ring_recv,
    pown_sem, psib_send, psib_recv, pring_send, pring_recv, all_send, all_recv, mate_send, mate_recv, last_sem,
):
    me, core, pos = ring_place(count)
    pairs = count // 2
    reach = pairs // 2
    rows = own.shape[2]
    other = me + 1 - 2 * core
    aims = (pair_at(pos + 1, count) * 2 + core, pair_at(pos - 1, count) * 2 + core)
    greet(aims + (other,))
    sent = []

    def launch(copy):
        copy.start()
        sent.append(copy)

    def band(rel, which, plane):
        owner = pair_at(pos + rel, count) * 2 + which
        return x_ref.at[plane, pl.ds(pl.multiple_of(owner * rows, rows), rows), :]

    def own_copy(rel, plane):
        return pltpu.make_async_copy(band(rel, core, plane), own.at[rel, plane], own_sem.at[rel, plane])

    def sib_copy(rel, plane):
        return remote(
            band(rel, 1 - core, plane), sib.at[rel, plane], sib_send.at[rel, plane], sib_recv.at[rel, plane], other
        )

    def pown_copy(rel):
        return pltpu.make_async_copy(
            probe_ref.at[:, pair_at(pos + rel, count), core], pown.at[rel], pown_sem.at[rel]
        )

    def psib_copy(rel):
        return remote(
            probe_ref.at[:, pair_at(pos + rel, count), 1 - core], psib.at[rel], psib_send.at[rel], psib_recv.at[rel],
            other,
        )

    order = [reach]
    for k in range(reach - 1, 0, -1):
        order += [k, pairs - k]
    order += [0]
    for rel in order[:1]:
        pown_copy(rel).start()
        launch(psib_copy(rel))
        for plane in range(2):
            own_copy(rel, plane).start()
            launch(sib_copy(rel, plane))
    for rel in order[1:]:
        pown_copy(rel).start()
        launch(psib_copy(rel))
    for rel in order[1:]:
        for plane in range(2):
            own_copy(rel, plane).start()
            launch(sib_copy(rel, plane))

    def ring_copy(way, rel, k, plane):
        return remote(
            own.at[rel, plane], inbox.at[way, k - 1, plane], ring_send.at[way, k - 1, plane],
            ring_recv.at[way, k - 1, plane], aims[way],
        )

    def add_rows(target, terms):
        block = 64

        def body(index, carry):
            at = pl.ds(pl.multiple_of(index * block, block), block)
            total = terms[0][at, :].astype(jnp.float32)
            for term in terms[1:]:
                total = total + term[at, :].astype(jnp.float32)
            target[at, :] = total.astype(target.dtype)
            return carry

        lax.fori_loop(0, rows // block, body, 0)

    def main_hop(way, k, plane):
        rel = k if way == 0 else pairs - k
        own_copy(rel, plane).wait()
        sib_copy(rel, plane).wait_recv()
        terms = [own.at[rel, plane], sib.at[rel, plane]]
        if k < reach and not (k == reach - 1 and plane != way):
            ring_copy(way, rel, k + 1, plane).wait_recv()
            terms.append(inbox.at[way, k, plane])
        add_rows(own.at[rel, plane], terms)
        launch(ring_copy(way, rel, k, plane))

    def pring_copy(way, rel, k):
        if k == reach:
            return remote(
                pown.at[rel, way], pinbox.at[way, k - 1, way], pring_send.at[way, k - 1], pring_recv.at[way, k - 1],
                aims[way],
            )
        return remote(
            pown.at[rel], pinbox.at[way, k - 1], pring_send.at[way, k - 1], pring_recv.at[way, k - 1], aims[way]
        )

    def probe_hop(k):
        if k == reach:
            pown_copy(reach).wait()
            psib_copy(reach).wait_recv()
            pown[reach] = pown[reach] + psib[reach]
            for way in range(2):
                launch(pring_copy(way, reach, k))
            return
        for way in range(2):
            rel = k if way == 0 else pairs - k
            pown_copy(rel).wait()
            psib_copy(rel).wait_recv()
            pring_copy(way, rel, k + 1).wait_recv()
            pown[rel] = pown[rel] + psib[rel]
            if k == reach - 1:
                pown[rel, way] = pown[rel, way] + pinbox[way, k, way]
            else:
                pown[rel] = pown[rel] + pinbox[way, k]
            launch(pring_copy(way, rel, k))

    def result(distance, which):
        return probe_out_ref.at[:, pair_at(pos + distance, count), which]

    def all_copy(src, way, hop, distance):
        if hop == reach - 1:
            place = probe_out_ref.at[way, pair_at(pos + distance, count), core]
        else:
            place = result(distance, core)
        return remote(src, place, all_send.at[way, hop], all_recv.at[way, hop], aims[way])

    def mate_copy(src, index, distance, which, plane=None):
        place = result(distance, which)
        if plane is not None:
            place = probe_out_ref.at[plane, pair_at(pos + distance, count), which]
        return remote(src, place, mate_send.at[index], mate_recv.at[index], other)

    last = pltpu.make_async_copy(pfinal, result(0, core), last_sem)

    def probe_finish():
        pown_copy(0).wait()
        psib_copy(0).wait_recv()
        total = pown[0] + psib[0]
        for way in range(2):
            pring_copy(way, 0, 1).wait_recv()
            total = total + pinbox[way, 0]
        pfinal[...] = total
        for way in range(2):
            launch(all_copy(pfinal, way, 0, 0))
        launch(mate_copy(pfinal, 0, 0, core))
        last.start()

    def probe_spread(hop):
        for way in range(2):
            distance = -(hop + 1) if way == 0 else hop + 1
            end = hop == reach - 1
            half = probe_out_ref.at[way, pair_at(pos + distance, count), core]
            here = half if end else result(distance, core)
            all_copy(here, way, hop, distance).wait_recv()
            if not end:
                launch(all_copy(half if hop == reach - 2 else here, way, hop + 1, distance))
            launch(mate_copy(here, 1 + 2 * hop + way, distance, core, way if end else None))

    stages = [functools.partial(probe_hop, k) for k in range(reach, 0, -1)]
    stages += [probe_finish]
    stages += [functools.partial(probe_spread, hop) for hop in range(reach)]
    hops = [[(0, reach, 0), (1, reach, 1)]]
    for k in range(reach - 1, 0, -1):
        for plane in range(2):
            hops.append([(0, k, 1 - plane), (1, k, plane)])
    while stages or hops:
        if stages:
            stages.pop(0)()
        if hops:
            for hop in hops.pop(0):
                main_hop(*hop)

    for plane in range(2):
        own_copy(0, plane).wait()
        sib_copy(0, plane).wait_recv()
        for way in range(2):
            ring_copy(way, 0, 1, plane).wait_recv()
        add_rows(
            out_ref.at[plane], [own.at[0, plane], sib.at[0, plane], inbox.at[0, 0, plane], inbox.at[1, 0, plane]]
        )
    mate_copy(result(0, 1 - core), 0, 0, 1 - core).wait_recv()
    for hop in range(reach):
        for way in range(2):
            distance = -(hop + 1) if way == 0 else hop + 1
            end = hop == reach - 1
            there = probe_out_ref.at[way, pair_at(pos + distance, count), 1 - core] if end else result(distance, 1 - core)
            mate_copy(there, 1 + 2 * hop + way, distance, 1 - core, way if end else None).wait_recv()
    last.wait()
    for copy in sent:
        copy.wait_send()


def reduce_steps(steps, probe_part, count):
    planes, long_rows, columns = steps.shape
    rows = long_rows // count
    pixels = probe_part.shape[1]
    pairs = count // 2
    reach = pairs // 2
    share = pixels // count
    dma = pltpu.SemaphoreType.DMA
    grad, total = pl.pallas_call(
        functools.partial(reduce_kernel, count),
        out_shape=(
            jax.ShapeDtypeStruct((planes, rows, columns), jnp.float32),
            jax.ShapeDtypeStruct((2, pairs, 2, share, pixels), jnp.float32),
        ),
        in_specs=[HBM, HBM],
        out_specs=(VMEM, ANY),
        scratch_shapes=[
            pltpu.VMEM((pairs, 2, rows, columns), jnp.bfloat16),
            pltpu.VMEM((pairs, 2, rows, columns), jnp.bfloat16),
            pltpu.VMEM((2, reach, 2, rows, columns), jnp.bfloat16),
            pltpu.VMEM((pairs, 2, share, pixels), jnp.float32),
            pltpu.VMEM((pairs, 2, share, pixels), jnp.float32),
            pltpu.VMEM((2, reach, 2, share, pixels), jnp.float32),
            pltpu.VMEM((2, share, pixels), jnp.float32),
            dma((pairs, 2)),
            dma((pairs, 2)),
            dma((pairs, 2)),
            dma((2, reach, 2)),
            dma((2, reach, 2)),
            dma((pairs,)),
            dma((pairs,)),
            dma((pairs,)),
            dma((2, reach)),
            dma((2, reach)),
            dma((2, reach)),
            dma((2, reach)),
            dma((2 * reach + 1,)),
            dma((2 * reach + 1,)),
            dma,
        ],
        compiler_params=pltpu.CompilerParams(
            collective_id=1, has_side_effects=True, vmem_limit_bytes=60 * 2**20
        ),
        name="reduce_steps",
    )(steps, probe_part.reshape(2, pairs, 2, share, pixels))
    return grad, total.reshape(2, pixels, pixels)


def on_device(object_field, probe_field, intensities, positions, live_counts):
    pixels = probe_field.shape[1]
    slots = positions.shape[2]
    count = lax.axis_size("scan")
    whole, blank = gather_object(object_field.astype(jnp.bfloat16), count)
    steps, probe_part = pattern_steps(
        whole,
        blank,
        probe_field,
        intensities.reshape(slots, pixels, pixels),
        positions.reshape(slots, 2),
        live_counts.reshape(1),
    )
    object_grad, probe_grad = reduce_steps(steps, probe_part, count)
    if lax.axis_size("sub") > 1:
        object_grad = lax.psum(object_grad, "sub")
    if lax.axis_size("obj") * lax.axis_size("sub") > 1:
        probe_grad = lax.psum(probe_grad, ("obj", "sub"))
    return (object_grad, probe_grad)


def solution(mesh):
    placed = (
        P(None, ("groups", "scan"), "obj"),
        P("groups", None, None),
        P(("groups", "obj"), "sub", "scan", None, None),
        P(("groups", "obj"), "sub", "scan", None),
        P(("groups", "obj"), "sub", "scan"),
    )
    return jax.shard_map(
        on_device,
        mesh=mesh,
        in_specs=placed,
        out_specs=(P(None, ("groups", "scan"), "obj"), P("groups", None, None)),
        check_vma=False,
    )
```

```python
import functools
import math

import jax
import jax.numpy as jnp
import numpy as np
from jax import lax
from jax.experimental import pallas as pl
from jax.experimental.pallas import tpu as pltpu
from jax.sharding import PartitionSpec as P

MESH = pl.DeviceIdType.MESH
ANY = pl.BlockSpec(memory_space=pl.ANY)
HBM = pl.BlockSpec(memory_space=pltpu.HBM)
VMEM = pl.BlockSpec(memory_space=pltpu.VMEM)
ROWS16 = 16


def ring_place(count):
    me = lax.axis_index("scan")
    core = lax.rem(me, 2)
    pair = me // 2
    pos = jnp.where(lax.rem(pair, 2) == 0, pair // 2, count // 2 - 1 - pair // 2)
    return me, core, pos


def pair_at(pos, count):
    pairs = count // 2
    pos = lax.rem(pos + 2 * pairs, pairs)
    return jnp.where(pos < pairs // 2, 2 * pos, 2 * (pairs - 1 - pos) + 1)


def greet(devices):
    barrier = pltpu.get_barrier_semaphore()
    for device in devices:
        pl.semaphore_signal(barrier, inc=1, device_id={"scan": device}, device_id_type=MESH)
    pl.semaphore_wait(barrier, len(devices))


def remote(src, dst, send_sem, recv_sem, device):
    return pltpu.make_async_remote_copy(
        src_ref=src,
        dst_ref=dst,
        send_sem=send_sem,
        recv_sem=recv_sem,
        device_id={"scan": device},
        device_id_type=MESH,
    )


def gather_kernel(count, x_ref, out_ref, zero_ref, zeros, ring_send, ring_recv, pair_send, pair_recv, own_sem, zero_sem):
    me, core, pos = ring_place(count)
    reach = count // 4
    rows = x_ref.shape[1]
    other = me + 1 - 2 * core
    aims = (pair_at(pos + 1, count) * 2 + core, pair_at(pos - 1, count) * 2 + core)
    greet(aims + (other,))

    def slot(distance, which, plane):
        owner = pair_at(pos + distance, count) * 2 + which
        return out_ref.at[plane, pl.ds(pl.multiple_of(owner * rows, rows), rows), :]

    sent = []

    def launch(copy):
        copy.start()
        sent.append(copy)

    def ring_copy(src, way, hop, plane, distance):
        return remote(
            src, slot(distance, core, plane), ring_send.at[way, hop, plane], ring_recv.at[way, hop, plane], aims[way]
        )

    def pair_copy(src, index, plane, distance, which):
        return remote(
            src, slot(distance, which, plane), pair_send.at[index, plane], pair_recv.at[index, plane], other
        )

    for plane in range(2):
        for way in range(2):
            launch(ring_copy(x_ref.at[plane], way, 0, plane, 0))
    for plane in range(2):
        launch(pair_copy(x_ref.at[plane], 0, plane, 0, core))
    own = [pltpu.make_async_copy(x_ref.at[plane], slot(0, core, plane), own_sem.at[plane]) for plane in range(2)]
    for copy in own:
        copy.start()
    zeros[...] = jnp.zeros_like(zeros)
    depth = zeros.shape[1]
    cleared = [
        pltpu.make_async_copy(zeros, zero_ref.at[:, pl.ds(part * depth, depth), :], zero_sem.at[part])
        for part in range(zero_ref.shape[1] // depth)
    ]
    for copy in cleared:
        copy.start()
    for hop in range(reach):
        for plane in range(2):
            for way in range(2):
                if hop == reach - 1 and plane != way:
                    continue
                distance = -(hop + 1) if way == 0 else hop + 1
                here = slot(distance, core, plane)
                ring_copy(here, way, hop, plane, distance).wait_recv()
                if hop < reach - 2 or (hop == reach - 2 and plane == way):
                    launch(ring_copy(here, way, hop + 1, plane, distance))
                index = 1 + 2 * hop + way
                launch(pair_copy(here, index, plane, distance, core))
    for plane in range(2):
        pair_copy(slot(0, 1 - core, plane), 0, plane, 0, 1 - core).wait_recv()
    for hop in range(reach):
        for plane in range(2):
            for way in range(2):
                if hop == reach - 1 and plane != way:
                    continue
                distance = -(hop + 1) if way == 0 else hop + 1
                index = 1 + 2 * hop + way
                pair_copy(slot(distance, 1 - core, plane), index, plane, distance, 1 - core).wait_recv()
    for copy in sent:
        copy.wait_send()
    for copy in own + cleared:
        copy.wait()


def gather_object(tile_low, count):
    planes, rows, columns = tile_low.shape
    whole = jax.ShapeDtypeStruct((planes, count * rows, columns), tile_low.dtype)
    reach = count // 4
    dma = pltpu.SemaphoreType.DMA
    return pl.pallas_call(
        functools.partial(gather_kernel, count),
        out_shape=(whole, whole),
        in_specs=[ANY],
        out_specs=(HBM, HBM),
        scratch_shapes=[
            pltpu.VMEM((planes, 2 * rows, columns), tile_low.dtype),
            dma((2, reach, 2)),
            dma((2, reach, 2)),
            dma((2 * reach + 1, 2)),
            dma((2 * reach + 1, 2)),
            dma((2,)),
            dma((count // 2,)),
        ],
        compiler_params=pltpu.CompilerParams(
            collective_id=0, has_side_effects=True, vmem_limit_bytes=16 * 2**20
        ),
        name="gather_object",
    )(tile_low)


def split(value):
    high = value.astype(jnp.bfloat16)
    return high, (value - high.astype(jnp.float32)).astype(jnp.bfloat16)


def product_left(table, value):
    first, second = split(value)
    terms = jnp.concatenate([first, first, second], axis=0)
    return jnp.dot(table[...], terms, preferred_element_type=jnp.float32)


def product_right(value, table):
    first, second = split(value)
    terms = jnp.concatenate([first, first, second], axis=1)
    return jnp.dot(terms, table[...], preferred_element_type=jnp.float32)


def halves(value, axis):
    middle = value.shape[axis] // 2
    if axis == 0:
        return value[:middle], value[middle:]
    return value[:, :middle], value[:, middle:]


def multiply(even, odd, tables, axis):
    found = []
    for table, parts in zip(tables, (even, odd)):
        stacked = jnp.concatenate([jnp.concatenate(part, axis=axis) for part in parts], axis=1 - axis)
        out = product_left(table, stacked) if axis == 0 else product_right(stacked, table)
        size = out.shape[1 - axis] // len(parts)
        planes = [
            out[:, index * size : (index + 1) * size] if axis == 0 else out[index * size : (index + 1) * size]
            for index in range(len(parts))
        ]
        found.append([halves(plane, axis) for plane in planes])
    return found


def ahead(waves, tables, axis):
    even, odd = [], []
    for wave in waves:
        split_parts = [halves(part, axis) for part in wave]
        even.append([first + second for first, second in split_parts])
        odd.append([first - second for first, second in split_parts])
    found = multiply(even, odd, tables, axis)
    return [
        tuple(jnp.concatenate([one, two], axis=axis) for one, two in zip(low, high)) for low, high in zip(*found)
    ]


def behind(waves, tables, axis):
    even = [[halves(part, axis)[0] for part in wave] for wave in waves]
    odd = [[halves(part, axis)[1] for part in wave] for wave in waves]
    found = multiply(even, odd, tables, axis)
    return [
        tuple(jnp.concatenate([one + two, one - two], axis=axis) for one, two in zip(low, high))
        for low, high in zip(*found)
    ]


def reorder(value, down, across):
    size = value.shape[0]
    first, second = split(value)
    both = jnp.dot(jnp.concatenate([first, second], axis=0), across, preferred_element_type=jnp.float32)
    both = both.astype(jnp.bfloat16)
    both = jnp.concatenate([both[:size], both[size:]], axis=1)
    both = jnp.dot(down, both, preferred_element_type=jnp.float32)
    return both[:, :size] + both[:, size:]


GROUP = 3


def pattern_kernel(
    place_ref, live_ref, probe_ref, measured_ref, down_ref, across_ref, *rest,
):
    tables, rest = rest[:8], rest[8:]
    (object_ref, blank_ref, steps_ref, sum_ref, windows, staged, in_sem, out_sem) = rest
    del blank_ref
    turn = pl.program_id(0)
    slots = windows.shape[0]
    group = measured_ref.shape[0]
    pixels = probe_ref.shape[1]
    tall = windows.shape[2]
    stripe = windows.shape[3]

    def aligned(index):
        return pl.multiple_of(place_ref[index, 0] // ROWS16 * ROWS16, ROWS16)

    def fetch(index):
        return pltpu.make_async_copy(
            object_ref.at[:, pl.ds(aligned(index), tall), :], windows.at[index], in_sem.at[index]
        )

    def emit(index):
        return pltpu.make_async_copy(
            staged.at[index], steps_ref.at[:, pl.ds(aligned(index), tall), :], out_sem.at[index]
        )

    @pl.when(turn == 0)
    def _():
        for index in range(slots):
            fetch(index).start()
        sum_ref[...] = jnp.zeros_like(sum_ref)

    for member in range(group):
        fetch(turn * group + member).wait()
    apart = lax.broadcasted_iota(jnp.int32, (stripe, pixels), 0) - lax.broadcasted_iota(
        jnp.int32, (stripe, pixels), 1
    )
    column_base = lax.axis_index("obj") * stripe
    picks, patches, waves = [], [], []
    probe_real = probe_ref[0]
    probe_imag = probe_ref[1]
    for member in range(group):
        slot = turn * group + member
        pick = jnp.where(apart == place_ref[slot, 1] - column_base, 1.0, 0.0).astype(jnp.bfloat16)
        both = jnp.concatenate([windows[slot, 0], windows[slot, 1]], axis=0)
        moved = jnp.dot(both, pick, preferred_element_type=jnp.float32)
        shift = lax.rem(tall - lax.rem(place_ref[slot, 0], ROWS16), tall)
        object_real = pltpu.roll(moved[:tall], shift, 0)[:pixels]
        object_imag = pltpu.roll(moved[tall:], shift, 0)[:pixels]
        picks.append(pick)
        patches.append((object_real, object_imag))
        waves.append(
            (
                probe_real * object_real - probe_imag * object_imag,
                probe_real * object_imag + probe_imag * object_real,
            )
        )
    far = ahead(ahead(waves, tables[0:2], 0), tables[2:4], 1)
    weighted = []
    for member in range(group):
        far_real, far_imag = far[member]
        misfit = far_real * far_real + far_imag * far_imag - reorder(
            measured_ref[member], down_ref[...], across_ref[...]
        )
        weighted.append((misfit * far_real, misfit * far_imag))
    back = behind(behind(weighted, tables[4:6], 0), tables[6:8], 1)
    total_real, total_imag = sum_ref[0], sum_ref[1]
    for member in range(group):
        slot = turn * group + member
        living = jnp.where(slot < live_ref[0], 1.0, 0.0).astype(jnp.float32)
        back_real, back_imag = back[member][0] * living, back[member][1] * living
        object_real, object_imag = patches[member]
        total_real += object_real * back_real + object_imag * back_imag
        total_imag += object_real * back_imag - object_imag * back_real
        row_off = lax.rem(place_ref[slot, 0], ROWS16)

        def shifted(value):
            low = value.astype(jnp.bfloat16).astype(jnp.float32)
            padded = jnp.concatenate([low, jnp.zeros((tall - pixels, pixels), jnp.float32)], axis=0)
            return pltpu.roll(padded, row_off, 0).astype(jnp.bfloat16)

        both = jnp.concatenate(
            [
                shifted(probe_real * back_real + probe_imag * back_imag),
                shifted(probe_real * back_imag - probe_imag * back_real),
            ],
            axis=0,
        )
        spread = lax.dot_general(both, picks[member], (((1,), (1,)), ((), ())), preferred_element_type=jnp.float32)
        spread = spread.astype(jnp.bfloat16)
        staged[slot, 0] = spread[:tall]
        staged[slot, 1] = spread[tall:]
        emit(slot).start()
    sum_ref[0] = total_real
    sum_ref[1] = total_imag

    @pl.when(turn == slots // group - 1)
    def _():
        for index in range(slots):
            emit(index).wait()


def dft_tables(pixels):
    half = pixels // 2
    order = np.concatenate([np.arange(0, pixels, 2), np.arange(1, pixels, 2)])
    down = np.eye(pixels, dtype=np.float32)[order]
    tables = [down.astype(jnp.bfloat16), np.ascontiguousarray(down.T).astype(jnp.bfloat16)]
    point = np.arange(half)
    kinds = []
    for odd in range(2):
        turns = (2 * point[:, None] + odd) * point[None, :] % pixels
        kinds.append(np.exp(-2j * math.pi * turns / pixels) / math.sqrt(pixels))
    for place in (lambda kind: kind, lambda kind: kind.T, lambda kind: kind.conj().T, lambda kind: kind.conj()):
        axis = (len(tables) // 2 + 1) % 2
        for kind in kinds:
            kind = place(kind)
            sign = 1 if axis else -1
            table = np.block([[kind.real, sign * kind.imag], [-sign * kind.imag, kind.real]]).astype(np.float32)
            high = table.astype(jnp.bfloat16)
            low = (table - high.astype(np.float32)).astype(jnp.bfloat16)
            tables.append(np.concatenate([high, low, high], axis=1 - axis))
    return tables


def pattern_steps(whole, blank, probe_field, measured, places, live):
    slots, pixels, _ = measured.shape
    stripe = whole.shape[2]
    tall = pixels + ROWS16
    group = GROUP if slots % GROUP == 0 else 1
    smem = pl.BlockSpec(memory_space=pltpu.SMEM)
    tables = dft_tables(pixels)
    plane = pl.BlockSpec((2, pixels, pixels), lambda turn: (0, 0, 0))
    return pl.pallas_call(
        pattern_kernel,
        grid=(slots // group,),
        out_shape=(
            jax.ShapeDtypeStruct(blank.shape, blank.dtype),
            jax.ShapeDtypeStruct(probe_field.shape, jnp.float32),
        ),
        in_specs=[
            smem, smem, plane, pl.BlockSpec((group, pixels, pixels), lambda turn: (turn, 0, 0)),
            *[pl.BlockSpec(table.shape, lambda turn: (0, 0)) for table in tables], HBM, HBM,
        ],
        out_specs=(HBM, plane),
        scratch_shapes=[
            pltpu.VMEM((slots, 2, tall, stripe), jnp.bfloat16),
            pltpu.VMEM((slots, 2, tall, stripe), jnp.bfloat16),
            pltpu.SemaphoreType.DMA((slots,)),
            pltpu.SemaphoreType.DMA((slots,)),
        ],
        input_output_aliases={5 + len(tables): 0},
        compiler_params=pltpu.CompilerParams(vmem_limit_bytes=60 * 2**20),
        name="pattern_steps",
    )(places, live, probe_field, measured, *tables, whole, blank)


def reduce_kernel(
    count, x_ref, probe_ref, out_ref, probe_out_ref, own, sib, inbox, pown, psib, pinbox, pfinal,
    own_sem, sib_send, sib_recv, ring_send, ring_recv,
    pown_sem, psib_send, psib_recv, pring_send, pring_recv, all_send, all_recv, mate_send, mate_recv, last_sem,
):
    me, core, pos = ring_place(count)
    pairs = count // 2
    reach = pairs // 2
    rows = own.shape[2]
    other = me + 1 - 2 * core
    aims = (pair_at(pos + 1, count) * 2 + core, pair_at(pos - 1, count) * 2 + core)
    greet(aims + (other,))
    sent = []

    def launch(copy):
        copy.start()
        sent.append(copy)

    def band(rel, which, plane):
        owner = pair_at(pos + rel, count) * 2 + which
        return x_ref.at[plane, pl.ds(pl.multiple_of(owner * rows, rows), rows), :]

    def own_copy(rel, plane):
        return pltpu.make_async_copy(band(rel, core, plane), own.at[rel, plane], own_sem.at[rel, plane])

    def sib_copy(rel, plane):
        return remote(
            band(rel, 1 - core, plane), sib.at[rel, plane], sib_send.at[rel, plane], sib_recv.at[rel, plane], other
        )

    def pown_copy(rel):
        return pltpu.make_async_copy(
            probe_ref.at[:, pair_at(pos + rel, count), core], pown.at[rel], pown_sem.at[rel]
        )

    def psib_copy(rel):
        return remote(
            probe_ref.at[:, pair_at(pos + rel, count), 1 - core], psib.at[rel], psib_send.at[rel], psib_recv.at[rel],
            other,
        )

    order = [reach]
    for k in range(reach - 1, 0, -1):
        order += [k, pairs - k]
    order += [0]
    for rel in order[:1]:
        pown_copy(rel).start()
        launch(psib_copy(rel))
        for plane in range(2):
            own_copy(rel, plane).start()
            launch(sib_copy(rel, plane))
    for rel in order[1:]:
        pown_copy(rel).start()
        launch(psib_copy(rel))
    for rel in order[1:]:
        for plane in range(2):
            own_copy(rel, plane).start()
            launch(sib_copy(rel, plane))

    def ring_copy(way, rel, k, plane):
        return remote(
            own.at[rel, plane], inbox.at[way, k - 1, plane], ring_send.at[way, k - 1, plane],
            ring_recv.at[way, k - 1, plane], aims[way],
        )

    def add_rows(target, terms):
        block = 64

        def body(index, carry):
            at = pl.ds(pl.multiple_of(index * block, block), block)
            total = terms[0][at, :].astype(jnp.float32)
            for term in terms[1:]:
                total = total + term[at, :].astype(jnp.float32)
            target[at, :] = total.astype(target.dtype)
            return carry

        lax.fori_loop(0, rows // block, body, 0)

    def main_hop(way, k, plane):
        rel = k if way == 0 else pairs - k
        own_copy(rel, plane).wait()
        sib_copy(rel, plane).wait_recv()
        terms = [own.at[rel, plane], sib.at[rel, plane]]
        if k < reach and not (k == reach - 1 and plane != way):
            ring_copy(way, rel, k + 1, plane).wait_recv()
            terms.append(inbox.at[way, k, plane])
        add_rows(own.at[rel, plane], terms)
        launch(ring_copy(way, rel, k, plane))

    def pring_copy(way, rel, k):
        if k == reach:
            return remote(
                pown.at[rel, way], pinbox.at[way, k - 1, way], pring_send.at[way, k - 1], pring_recv.at[way, k - 1],
                aims[way],
            )
        return remote(
            pown.at[rel], pinbox.at[way, k - 1], pring_send.at[way, k - 1], pring_recv.at[way, k - 1], aims[way]
        )

    def probe_hop(k):
        if k == reach:
            pown_copy(reach).wait()
            psib_copy(reach).wait_recv()
            pown[reach] = pown[reach] + psib[reach]
            for way in range(2):
                launch(pring_copy(way, reach, k))
            return
        for way in range(2):
            rel = k if way == 0 else pairs - k
            pown_copy(rel).wait()
            psib_copy(rel).wait_recv()
            pring_copy(way, rel, k + 1).wait_recv()
            pown[rel] = pown[rel] + psib[rel]
            if k == reach - 1:
                pown[rel, way] = pown[rel, way] + pinbox[way, k, way]
            else:
                pown[rel] = pown[rel] + pinbox[way, k]
            launch(pring_copy(way, rel, k))

    def result(distance, which):
        return probe_out_ref.at[:, pair_at(pos + distance, count), which]

    def all_copy(src, way, hop, distance):
        if hop == reach - 1:
            place = probe_out_ref.at[way, pair_at(pos + distance, count), core]
        else:
            place = result(distance, core)
        return remote(src, place, all_send.at[way, hop], all_recv.at[way, hop], aims[way])

    def mate_copy(src, index, distance, which, plane=None):
        place = result(distance, which)
        if plane is not None:
            place = probe_out_ref.at[plane, pair_at(pos + distance, count), which]
        return remote(src, place, mate_send.at[index], mate_recv.at[index], other)

    last = pltpu.make_async_copy(pfinal, result(0, core), last_sem)

    def probe_finish():
        pown_copy(0).wait()
        psib_copy(0).wait_recv()
        total = pown[0] + psib[0]
        for way in range(2):
            pring_copy(way, 0, 1).wait_recv()
            total = total + pinbox[way, 0]
        pfinal[...] = total
        for way in range(2):
            launch(all_copy(pfinal, way, 0, 0))
        launch(mate_copy(pfinal, 0, 0, core))
        last.start()

    def probe_spread(hop):
        for way in range(2):
            distance = -(hop + 1) if way == 0 else hop + 1
            end = hop == reach - 1
            half = probe_out_ref.at[way, pair_at(pos + distance, count), core]
            here = half if end else result(distance, core)
            all_copy(here, way, hop, distance).wait_recv()
            if not end:
                launch(all_copy(half if hop == reach - 2 else here, way, hop + 1, distance))
            launch(mate_copy(here, 1 + 2 * hop + way, distance, core, way if end else None))

    stages = [functools.partial(probe_hop, k) for k in range(reach, 0, -1)]
    stages += [probe_finish]
    stages += [functools.partial(probe_spread, hop) for hop in range(reach)]
    hops = [[(0, reach, 0), (1, reach, 1)]]
    for k in range(reach - 1, 0, -1):
        for plane in range(2):
            hops.append([(0, k, 1 - plane), (1, k, plane)])
    while stages or hops:
        if stages:
            stages.pop(0)()
        if hops:
            for hop in hops.pop(0):
                main_hop(*hop)

    for plane in range(2):
        own_copy(0, plane).wait()
        sib_copy(0, plane).wait_recv()
        for way in range(2):
            ring_copy(way, 0, 1, plane).wait_recv()
        add_rows(
            out_ref.at[plane], [own.at[0, plane], sib.at[0, plane], inbox.at[0, 0, plane], inbox.at[1, 0, plane]]
        )
    mate_copy(result(0, 1 - core), 0, 0, 1 - core).wait_recv()
    for hop in range(reach):
        for way in range(2):
            distance = -(hop + 1) if way == 0 else hop + 1
            end = hop == reach - 1
            there = probe_out_ref.at[way, pair_at(pos + distance, count), 1 - core] if end else result(distance, 1 - core)
            mate_copy(there, 1 + 2 * hop + way, distance, 1 - core, way if end else None).wait_recv()
    last.wait()
    for copy in sent:
        copy.wait_send()


def reduce_steps(steps, probe_part, count):
    planes, long_rows, columns = steps.shape
    rows = long_rows // count
    pixels = probe_part.shape[1]
    pairs = count // 2
    reach = pairs // 2
    share = pixels // count
    dma = pltpu.SemaphoreType.DMA
    grad, total = pl.pallas_call(
        functools.partial(reduce_kernel, count),
        out_shape=(
            jax.ShapeDtypeStruct((planes, rows, columns), jnp.float32),
            jax.ShapeDtypeStruct((2, pairs, 2, share, pixels), jnp.float32),
        ),
        in_specs=[HBM, HBM],
        out_specs=(VMEM, ANY),
        scratch_shapes=[
            pltpu.VMEM((pairs, 2, rows, columns), jnp.bfloat16),
            pltpu.VMEM((pairs, 2, rows, columns), jnp.bfloat16),
            pltpu.VMEM((2, reach, 2, rows, columns), jnp.bfloat16),
            pltpu.VMEM((pairs, 2, share, pixels), jnp.float32),
            pltpu.VMEM((pairs, 2, share, pixels), jnp.float32),
            pltpu.VMEM((2, reach, 2, share, pixels), jnp.float32),
            pltpu.VMEM((2, share, pixels), jnp.float32),
            dma((pairs, 2)),
            dma((pairs, 2)),
            dma((pairs, 2)),
            dma((2, reach, 2)),
            dma((2, reach, 2)),
            dma((pairs,)),
            dma((pairs,)),
            dma((pairs,)),
            dma((2, reach)),
            dma((2, reach)),
            dma((2, reach)),
            dma((2, reach)),
            dma((2 * reach + 1,)),
            dma((2 * reach + 1,)),
            dma,
        ],
        compiler_params=pltpu.CompilerParams(
            collective_id=1, has_side_effects=True, vmem_limit_bytes=24 * 2**20
        ),
        name="reduce_steps",
    )(steps, probe_part.reshape(2, pairs, 2, share, pixels))
    return grad, total.reshape(2, pixels, pixels)


def on_device(object_field, probe_field, intensities, positions, live_counts):
    pixels = probe_field.shape[1]
    slots = positions.shape[2]
    count = lax.axis_size("scan")
    whole, blank = gather_object(object_field.astype(jnp.bfloat16), count)
    steps, probe_part = pattern_steps(
        whole,
        blank,
        probe_field,
        intensities.reshape(slots, pixels, pixels),
        positions.reshape(slots, 2),
        live_counts.reshape(1),
    )
    object_grad, probe_grad = reduce_steps(steps, probe_part, count)
    if lax.axis_size("sub") > 1:
        object_grad = lax.psum(object_grad, "sub")
    if lax.axis_size("obj") * lax.axis_size("sub") > 1:
        probe_grad = lax.psum(probe_grad, ("obj", "sub"))
    return (object_grad, probe_grad)


def solution(mesh):
    placed = (
        P(None, ("groups", "scan"), "obj"),
        P("groups", None, None),
        P(("groups", "obj"), "sub", "scan", None, None),
        P(("groups", "obj"), "sub", "scan", None),
        P(("groups", "obj"), "sub", "scan"),
    )
    return jax.shard_map(
        on_device,
        mesh=mesh,
        in_specs=placed,
        out_specs=(P(None, ("groups", "scan"), "obj"), P("groups", None, None)),
        check_vma=False,
    )
```
